32 devices in a mesh: seq: 8 (over y, x, core), tp: 4 (over z).
Axes of the slice: x: 2, y: 2, z: 4, core: 2. Of those that a mesh axis runs over, the one named last changes fastest.
Arguments:
- query_heads: bfloat16 [4096, 2048], P('seq', 'tp'), may hold values from -120 to 120
- key_heads: bfloat16 [4096, 2048], P('seq', 'tp'), may hold values from -120 to 120
- value_heads: bfloat16 [4096, 2048], P('seq', 'tp'), may hold values from -6 to 6
- out_weight: bfloat16 [2048, 2048], P('tp'), may hold values from -0.125 to 0.125
- cotangent: bfloat16 [4096, 2048], P('seq', 'tp'), may hold values from -6 to 6
- loss_mask: int32 [4096], P('seq'), may hold values 0 or 1
- block_pattern: int32 [16, 9], replicated, may hold values from 0 to 15, as said below
- block_counts: int32 [16], replicated, may hold values from 1 to 9
Outputs:
- attended: bfloat16 [4096, 2048], P('seq', 'tp')
- query_grad: bfloat16 [4096, 2048], P('seq', 'tp')
- key_grad: bfloat16 [4096, 2048], P('seq', 'tp')
- value_grad: bfloat16 [4096, 2048], P('seq', 'tp')
- weight_grad: float32 [2048, 2048], P('tp', 'seq')
The draws below stay inside these ranges and needn't reach their ends.
Inputs may be any that keep to these rules, and one draw needn't show every extreme that they name: For j < block_counts[b], block_pattern[b, j] are distinct blocks within 4 of b, the first being b itself; later entries are ignored.
All inputs are finite; a program needn't handle non-finite values. No bound on the sum of `loss_mask` on one device may be relied on, other than what follows from the above.
Results may differ from the reference program's by a relative error of at most 0.035.
Values may be sent and summed in bfloat16 or wider, within the bound.
A program may use at most 192 MiB of HBM per device.

```python
import math
import jax
import jax.numpy as jnp
from jax import lax

D = 2048
HEADS = 16
HD = 128
BLK = 256
WINDOW = 4
LIST = 9
SEQ = 4096
NBLK = 16


def block_lists(shared_key):
    seed_order, seed_count = jax.random.split(jax.random.fold_in(shared_key, 11))
    offsets = jnp.concatenate([jnp.arange(-WINDOW, 0), jnp.arange(1, WINDOW + 1)]).astype(jnp.int32)
    query_ids = jnp.arange(NBLK, dtype=jnp.int32)[:, None]
    targets = query_ids + offsets[None, :]
    inside = (targets >= 0) & (targets < NBLK)
    ranks = jax.random.randint(seed_order, (NBLK, 2 * WINDOW), 0, 1 << 20) * (2 * WINDOW) + jnp.arange(2 * WINDOW, dtype=jnp.int32)[None, :]
    ranks = jnp.where(inside, ranks, ranks + (1 << 28))
    ordering = jnp.argsort(ranks, axis=1, stable=True)
    ordered = jnp.take_along_axis(targets, ordering, axis=1)
    ordered_in = jnp.take_along_axis(inside, ordering, axis=1)
    pattern = jnp.concatenate([query_ids, jnp.where(ordered_in, ordered, query_ids)], axis=1).astype(jnp.int32)
    available = 1 + jnp.sum(inside.astype(jnp.int32), axis=1)
    raw_count = jax.random.randint(seed_count, (NBLK,), 0, 1 << 20) % available
    counts = raw_count * raw_count // jnp.maximum(available - 1, 1) + 1
    counts = jnp.where(query_ids[:, 0] == WINDOW, available, counts).astype(jnp.int32)
    return (pattern, counts)


def draw_block_pattern(key, part):
    shared = block_lists(key)
    return shared[0]


def draw_block_counts(key, part):
    shared = block_lists(key)
    return shared[1]


def draw_query_heads(key, part):
    key = jax.random.fold_in(key, 5)
    values = jnp.clip(jax.random.normal(key, (SEQ, D), jnp.float32), -6.0, 6.0)
    return values.astype(jnp.bfloat16)


def draw_key_heads(key, part):
    key = jax.random.fold_in(key, 6)
    values = jnp.clip(jax.random.normal(key, (SEQ, D), jnp.float32), -6.0, 6.0)
    return values.astype(jnp.bfloat16)


def set_ends(values, own_key, least, largest):
    index_at = [jax.random.randint(jax.random.fold_in(own_key, axis), (), 0, length) for axis, length in enumerate(values.shape)]
    main_axis = values.shape.index(max(values.shape))
    beside = index_at[:main_axis] + [(index_at[main_axis] + 1) % values.shape[main_axis]] + index_at[main_axis + 1:]
    return values.at[tuple(index_at)].set(least).at[tuple(beside)].set(largest)


def block_levels(key, dims, pieces, low, largest):
    gain = 1.0
    for dim, blocks in pieces:
        steps = jax.random.uniform(jax.random.fold_in(jax.random.fold_in(key, 6), dim), (blocks,), jnp.float32, low / len(pieces), largest / len(pieces))
        gain = gain * jnp.repeat(jnp.exp(steps), dims[dim] // blocks).reshape((-1,) + (1,) * (len(dims) - 1 - dim))
    return gain


def gaussian(rng, shape, scale, reach, cuts=(), held_as=jnp.bfloat16):
    array = scale * jax.random.normal(rng, shape, jnp.float32)
    if cuts:
        array = array * block_levels(rng, shape, cuts, -0.22, 0.18)
    return jnp.clip(array, -reach, reach).astype(held_as)


def setup_inputs(seed: int = 0) -> dict:
    streams_of = jax.random.split(jax.random.key(seed), 9)
    return {
        "query_heads": draw_query_heads(jax.random.fold_in(streams_of[8], 71), 0),
        "key_heads": draw_key_heads(jax.random.fold_in(streams_of[8], 71), 0),
        "value_heads": gaussian(streams_of[2], (SEQ, HEADS * HD), 1.0, 6.0, ((0, 8), (1, 4))),
        "out_weight": gaussian(streams_of[3], (HEADS * HD, D), (HEADS * HD) ** -0.5, 0.125, ((0, 4),)),
        "cotangent": gaussian(streams_of[4], (SEQ, D), 1.0, 6.0, ((0, 8), (1, 4))),
        "loss_mask": set_ends((jax.random.randint(streams_of[5], (SEQ,), 0, 2) < 1).astype(jnp.int32), jax.random.fold_in(streams_of[5], 1), 0, 1),
        "block_pattern": draw_block_pattern(jax.random.fold_in(streams_of[8], 71), 0),
        "block_counts": draw_block_counts(jax.random.fold_in(streams_of[8], 71), 0),
    }


def take_blocks(source, block_ids):

    def one_block(block_id):
        return lax.dynamic_slice_in_dim(source, (block_id * BLK).astype(jnp.int32), BLK, 0)
    return jax.vmap(one_block)(block_ids).reshape(LIST, BLK, HEADS, HD).astype(jnp.float32)

def block_scores(query_block, key_blocks, listed):
    logits = jnp.einsum('qhd,lkhd->hqlk', query_block, key_blocks) * (1.0 / math.sqrt(HD))
    return jnp.where(listed[None, None, :, None], logits, -jnp.inf)

def reference(query_heads, key_heads, value_heads, out_weight, cotangent, loss_mask, block_pattern, block_counts):
    slot_live = jnp.arange(LIST, dtype=jnp.int32)[None, :] < block_counts[:, None]
    block_range = jnp.arange(NBLK, dtype=jnp.int32)

    def forward_block(block_id):
        block_ids = block_pattern[block_id]
        listed = slot_live[block_id]
        row_start = (block_id * BLK).astype(jnp.int32)
        query_block = lax.dynamic_slice_in_dim(query_heads, row_start, BLK, 0).reshape(BLK, HEADS, HD).astype(jnp.float32)
        logits = block_scores(query_block, take_blocks(key_heads, block_ids), listed)
        highest = lax.optimization_barrier(jnp.max(logits, axis=(2, 3), keepdims=True))
        log_total = highest + jnp.log(lax.optimization_barrier(jnp.sum(jnp.exp(logits - highest), axis=(2, 3), keepdims=True)))
        weights = lax.optimization_barrier(jnp.exp(logits - log_total).astype(jnp.bfloat16)).astype(jnp.float32)
        blended = jnp.einsum('hqlk,lkhd->qhd', weights, take_blocks(value_heads, block_ids))
        return (blended.reshape(BLK, HEADS * HD).astype(jnp.bfloat16), log_total[:, :, 0, 0])
    heads_out, log_totals = lax.map(forward_block, block_range)
    heads_out = heads_out.reshape(SEQ, HEADS * HD)
    attended = jnp.dot(heads_out, out_weight, preferred_element_type=jnp.float32).astype(jnp.bfloat16)
    masked = jnp.where(loss_mask[:, None] == 1, cotangent, jnp.zeros_like(cotangent))
    weight_grad = jnp.dot(heads_out.T, masked, preferred_element_type=jnp.float32)
    d_heads = jnp.dot(masked, out_weight.T, preferred_element_type=jnp.float32).astype(jnp.bfloat16)
    row_dots = lax.optimization_barrier(jnp.sum((d_heads.astype(jnp.float32) * heads_out.astype(jnp.float32)).reshape(SEQ, HEADS, HD), axis=2))

    def backward_block(carried, block_id):
        key_acc, value_acc = carried
        block_ids = block_pattern[block_id]
        listed = slot_live[block_id]
        row_start = (block_id * BLK).astype(jnp.int32)
        query_block = lax.dynamic_slice_in_dim(query_heads, row_start, BLK, 0).reshape(BLK, HEADS, HD).astype(jnp.float32)
        grad_block = lax.dynamic_slice_in_dim(d_heads, row_start, BLK, 0).reshape(BLK, HEADS, HD).astype(jnp.float32)
        dots_block = lax.dynamic_slice_in_dim(row_dots, row_start, BLK, 0).T
        key_blocks = take_blocks(key_heads, block_ids)
        value_blocks = take_blocks(value_heads, block_ids)
        logits = block_scores(query_block, key_blocks, listed)
        weights = jnp.exp(logits - log_totals[block_id][:, :, None, None])
        weights_b = lax.optimization_barrier(weights.astype(jnp.bfloat16)).astype(jnp.float32)
        d_probs = jnp.einsum('qhd,lkhd->hqlk', grad_block, value_blocks)
        d_logits = weights * (d_probs - dots_block[:, :, None, None]) * (1.0 / math.sqrt(HD))
        d_logits = lax.optimization_barrier(d_logits.astype(jnp.bfloat16)).astype(jnp.float32)
        query_grad = jnp.einsum('hqlk,lkhd->qhd', d_logits, key_blocks).reshape(BLK, HEADS * HD).astype(jnp.bfloat16)
        key_parts = jnp.einsum('hqlk,qhd->lkhd', d_logits, query_block).reshape(LIST, BLK, HEADS * HD)
        value_parts = jnp.einsum('hqlk,qhd->lkhd', weights_b, grad_block).reshape(LIST, BLK, HEADS * HD)
        for slot_id in range(LIST):
            block_row = (block_ids[slot_id] * BLK).astype(jnp.int32)
            key_acc = lax.dynamic_update_slice_in_dim(key_acc, lax.dynamic_slice_in_dim(key_acc, block_row, BLK, 0) + key_parts[slot_id], block_row, 0)
            value_acc = lax.dynamic_update_slice_in_dim(value_acc, lax.dynamic_slice_in_dim(value_acc, block_row, BLK, 0) + value_parts[slot_id], block_row, 0)
        return ((key_acc, value_acc), query_grad)
    zero_acc = jnp.zeros((SEQ, HEADS * HD), jnp.float32)
    (key_acc, value_acc), query_grads = lax.scan(backward_block, (zero_acc, zero_acc), block_range)
    query_grad = query_grads.reshape(SEQ, HEADS * HD)
    return (attended, query_grad, key_acc.astype(jnp.bfloat16), value_acc.astype(jnp.bfloat16), weight_grad)
```

```python
import math

import jax
import jax.numpy as jnp
from jax import lax
from jax.experimental import pallas as pl
from jax.experimental.pallas import tpu as pltpu
from jax.sharding import PartitionSpec as P

HD = 128
BLK = 256
WINDOW = 4


FLOOR_LOGIT = -1e30
SCALE = 1.0 / math.sqrt(HD)
LOG2_SCALE = SCALE * math.log2(math.e)
NT = (((1,), (1,)), ((), ()))
TN = (((0,), (0,)), ((), ()))
VMEM_LIMIT = 48 * 1024 * 1024


def passed_along(value, axis, steps):
    count = lax.axis_size(axis)
    leading, last = (max(0, -steps), min(count, count - steps))
    return lax.ppermute(value, axis, [(source, source + steps) for source in range(leading, last)])


def listed_table(block_pattern, block_counts, query_first, query_count, key_first, key_count):
    query_lists = lax.dynamic_slice_in_dim(block_pattern, query_first, query_count, 0)
    list_sizes = lax.dynamic_slice_in_dim(block_counts, query_first, query_count, 0)
    slot_ids = jnp.arange(block_pattern.shape[1], dtype=jnp.int32)
    in_use = slot_ids[None, :] < list_sizes[:, None]
    key_ids = key_first + jnp.arange(key_count, dtype=jnp.int32)
    matched = (query_lists[:, :, None] == key_ids[None, None, :]) & in_use[:, :, None]
    return jnp.any(matched, axis=1)


def masked_logits(query_part, key_part, listed):
    logits = jnp.einsum(
        "qhd,khd->hqk", query_part, key_part, preferred_element_type=jnp.float32
    ) * (1.0 / math.sqrt(HD))
    head_count, query_len, key_len = logits.shape
    blocked = logits.reshape(
        head_count,
        listed.shape[0],
        query_len // listed.shape[0],
        listed.shape[1],
        key_len // listed.shape[1],
    )
    blocked = jnp.where(listed[None, :, None, :, None], blocked, FLOOR_LOGIT)
    return blocked.reshape(head_count, query_len, key_len)


def piece_logits(query_part, key_part, listed):

    def compute(unused):
        return masked_logits(query_part, key_part, listed)

    def skipped(unused):
        return jnp.full(
            (query_part.shape[1], query_part.shape[0], key_part.shape[0]), FLOOR_LOGIT, jnp.float32
        )

    return lax.cond(jnp.any(listed), compute, skipped, 0)


def piece_output(logits, log_total, value_part, listed):

    def compute(unused):
        weights_b = jnp.exp(logits - log_total[:, :, None]).astype(jnp.bfloat16)
        return jnp.einsum("hqk,khd->hqd", weights_b, value_part, preferred_element_type=jnp.float32)

    def skipped(unused):
        return jnp.zeros((logits.shape[0], logits.shape[1], value_part.shape[2]), jnp.float32)

    return lax.cond(jnp.any(listed), compute, skipped, 0)


def pair_terms(
    logits,
    query_part,
    grad_part,
    log_total,
    row_dots,
    key_part,
    value_part,
    listed,
    want_query,
    want_keys,
):
    query_shape = query_part.shape
    key_shape = key_part.shape

    def compute(unused):
        scores = masked_logits(query_part, key_part, listed) if logits is None else logits
        weights = jnp.exp(scores - log_total[:, :, None])
        d_probs = jnp.einsum(
            "qhd,khd->hqk", grad_part, value_part, preferred_element_type=jnp.float32
        )
        d_logits = (weights * (d_probs - row_dots[:, :, None]) * (1.0 / math.sqrt(HD))).astype(
            jnp.bfloat16
        )
        query_term = jnp.zeros(query_shape, jnp.float32)
        key_term = jnp.zeros(key_shape, jnp.float32)
        value_term = jnp.zeros(key_shape, jnp.float32)
        if want_query:
            query_term = jnp.einsum(
                "hqk,khd->qhd", d_logits, key_part, preferred_element_type=jnp.float32
            )
        if want_keys:
            key_term = jnp.einsum(
                "hqk,qhd->khd", d_logits, query_part, preferred_element_type=jnp.float32
            )
            value_term = jnp.einsum(
                "hqk,qhd->khd",
                weights.astype(jnp.bfloat16),
                grad_part,
                preferred_element_type=jnp.float32,
            )
        return (query_term, key_term, value_term)

    def skipped(unused):
        return (
            jnp.zeros(query_shape, jnp.float32),
            jnp.zeros(key_shape, jnp.float32),
            jnp.zeros(key_shape, jnp.float32),
        )

    return lax.cond(jnp.any(listed), compute, skipped, 0)


def local(
    query_heads,
    key_heads,
    value_heads,
    out_weight,
    cotangent,
    loss_mask,
    block_pattern,
    block_counts,
):
    tok_rows = query_heads.shape[0]
    local_cols = query_heads.shape[1]
    head_count = local_cols // HD
    query_blocks = tok_rows // BLK
    seq_devices = lax.axis_size("seq")
    reach_dev = min((WINDOW * BLK + tok_rows - 1) // tok_rows, seq_devices - 1)
    position = lax.axis_index("seq")
    own_first = position * query_blocks
    query_part = query_heads.reshape(tok_rows, head_count, HD)
    offsets = [distance for distance in range(-reach_dev, reach_dev + 1) if distance != 0]
    neighbours = []
    for distance in offsets:
        arrived = passed_along((key_heads, value_heads), "seq", distance)
        neighbours.append((position - distance, arrived[0], arrived[1]))
    pieces = [(position, key_heads, value_heads)] + neighbours
    prepared = []
    for source, key_piece, value_piece in pieces:
        listed = listed_table(
            block_pattern,
            block_counts,
            own_first,
            query_blocks,
            source * query_blocks,
            query_blocks,
        )
        key_part = key_piece.reshape(tok_rows, head_count, HD)
        value_part = value_piece.reshape(tok_rows, head_count, HD)
        prepared.append((listed, key_part, value_part, piece_logits(query_part, key_part, listed)))
    highest = jnp.full((head_count, tok_rows), FLOOR_LOGIT, jnp.float32)
    for listed, key_part, value_part, logits in prepared:
        highest = jnp.maximum(highest, jnp.max(logits, axis=2))
    denominator = jnp.zeros((head_count, tok_rows), jnp.float32)
    for listed, key_part, value_part, logits in prepared:
        denominator = denominator + jnp.sum(jnp.exp(logits - highest[:, :, None]), axis=2)
    log_total = highest + jnp.log(denominator)
    weighted = jnp.zeros((head_count, tok_rows, HD), jnp.float32)
    for listed, key_part, value_part, logits in prepared:
        weighted = weighted + piece_output(logits, log_total, value_part, listed)
    heads_out = (
        jnp.transpose(weighted, (1, 0, 2)).reshape(tok_rows, local_cols).astype(jnp.bfloat16)
    )
    partial_out = jnp.dot(heads_out, out_weight, preferred_element_type=jnp.float32)
    attended = lax.psum_scatter(partial_out, "tp", scatter_dimension=1, tiled=True).astype(
        jnp.bfloat16
    )
    masked = jnp.where(loss_mask[:, None] == 1, cotangent, jnp.zeros_like(cotangent))
    full_grad = lax.all_gather(masked, "tp", axis=1, tiled=True)
    weight_part = jnp.einsum("tc,td->cd", heads_out, full_grad, preferred_element_type=jnp.float32)
    weight_grad = lax.psum_scatter(weight_part, "seq", scatter_dimension=1, tiled=True)
    d_heads = jnp.einsum(
        "td,cd->tc", full_grad, out_weight, preferred_element_type=jnp.float32
    ).astype(jnp.bfloat16)
    grad_part = d_heads.reshape(tok_rows, head_count, HD)
    row_dots = jnp.sum(
        grad_part.astype(jnp.float32)
        * heads_out.reshape(tok_rows, head_count, HD).astype(jnp.float32),
        axis=2,
    ).T
    own_listed, own_keys, own_values, own_logits = prepared[0]
    term_set = pair_terms(
        own_logits,
        query_part,
        grad_part,
        log_total,
        row_dots,
        own_keys,
        own_values,
        own_listed,
        True,
        True,
    )
    query_acc, key_acc, value_acc = term_set
    for listed, key_part, value_part, logits in prepared[1:]:
        term_set = pair_terms(
            logits,
            query_part,
            grad_part,
            log_total,
            row_dots,
            key_part,
            value_part,
            listed,
            True,
            False,
        )
        query_acc = query_acc + term_set[0]
    for distance in offsets:
        arrived = passed_along((query_heads, d_heads), "seq", distance)
        arrived_stats = passed_along((log_total, row_dots), "seq", distance)
        sender = position - distance
        inside = (sender >= 0) & (sender < seq_devices)
        listed = (
            listed_table(
                block_pattern,
                block_counts,
                sender * query_blocks,
                query_blocks,
                own_first,
                query_blocks,
            )
            & inside
        )
        term_set = pair_terms(
            None,
            arrived[0].reshape(tok_rows, head_count, HD),
            arrived[1].reshape(tok_rows, head_count, HD),
            arrived_stats[0],
            arrived_stats[1],
            own_keys,
            own_values,
            listed,
            False,
            True,
        )
        key_acc = key_acc + term_set[1]
        value_acc = value_acc + term_set[2]
    query_grad = query_acc.reshape(tok_rows, local_cols).astype(jnp.bfloat16)
    key_grad = key_acc.reshape(tok_rows, local_cols).astype(jnp.bfloat16)
    value_grad = value_acc.reshape(tok_rows, local_cols).astype(jnp.bfloat16)
    return (attended, query_grad, key_grad, value_grad, weight_grad)


def block_slot(block, parity):
    return (((block // 2) + parity) % 2) * 8 + (block // 4) * 2 + block % 2


def forward_kernel(pattern, counts, parity_ref, q_ref, k_ref, v_ref, out_ref, total_ref, scores):
    parity = parity_ref[0]

    def query_block(index, carry):
        block = 4 * (index // 2) + 2 * parity + index % 2
        entries = counts[block]
        query = q_ref[index]

        def score(entry, highest):
            slot = block_slot(pattern[block, entry], parity)
            logits = (
                lax.dot_general(k_ref[slot], query, NT, preferred_element_type=jnp.float32)
                * LOG2_SCALE
            )
            scores[entry] = logits
            return jnp.maximum(highest, jnp.max(logits, axis=0, keepdims=True))

        highest = lax.fori_loop(0, entries, score, jnp.full((1, BLK), FLOOR_LOGIT, jnp.float32))

        def blend(entry, state):
            total, mixed = state
            slot = block_slot(pattern[block, entry], parity)
            weights = jnp.exp2(scores[entry] - highest)
            total = total + jnp.sum(weights, axis=0, keepdims=True)
            mixed = mixed + lax.dot_general(
                v_ref[slot], weights.astype(jnp.bfloat16), TN, preferred_element_type=jnp.float32
            )
            return total, mixed

        total, mixed = lax.fori_loop(
            0,
            entries,
            blend,
            (jnp.zeros((1, BLK), jnp.float32), jnp.zeros((HD, BLK), jnp.float32)),
        )
        out_ref[index] = jnp.transpose(mixed / total).astype(jnp.bfloat16)
        total_ref[index] = highest + jnp.log2(total)
        return carry

    lax.fori_loop(0, q_ref.shape[0], query_block, 0)


def backward_kernel(
    pattern,
    counts,
    parity_ref,
    q_ref,
    k_ref,
    v_ref,
    out_ref,
    total_ref,
    grad_ref,
    dq_ref,
    dk_ref,
    dv_ref,
    dk_far_ref,
    dv_far_ref,
    dk_acc,
    dv_acc,
):
    parity = parity_ref[0]
    dk_acc[...] = jnp.zeros_like(dk_acc)
    dv_acc[...] = jnp.zeros_like(dv_acc)

    def query_block(index, carry):
        block = 4 * (index // 2) + 2 * parity + index % 2
        query = q_ref[index]
        grad = grad_ref[index]
        log_total = total_ref[index]
        products = grad.astype(jnp.float32) * out_ref[index].astype(jnp.float32)
        row_dots = jnp.sum(jnp.transpose(products), axis=0, keepdims=True)

        def pair(entry, dq):
            slot = block_slot(pattern[block, entry], parity)
            key = k_ref[slot]
            logits = (
                lax.dot_general(key, query, NT, preferred_element_type=jnp.float32) * LOG2_SCALE
            )
            weights = jnp.exp2(logits - log_total)
            d_probs = lax.dot_general(v_ref[slot], grad, NT, preferred_element_type=jnp.float32)
            d_logits = (weights * (d_probs - row_dots)).astype(jnp.bfloat16)
            dv_acc[slot] += jnp.dot(
                weights.astype(jnp.bfloat16), grad, preferred_element_type=jnp.float32
            )
            dk_acc[slot] += jnp.dot(d_logits, query, preferred_element_type=jnp.float32)
            return dq + lax.dot_general(key, d_logits, TN, preferred_element_type=jnp.float32)

        dq = lax.fori_loop(0, counts[block], pair, jnp.zeros((HD, BLK), jnp.float32))
        dq_ref[index] = jnp.transpose(dq * SCALE).astype(jnp.bfloat16)
        return carry

    lax.fori_loop(0, q_ref.shape[0], query_block, 0)
    half = dk_acc.shape[0] // 2
    dk_ref[...] = dk_acc[:half] * SCALE
    dv_ref[...] = dv_acc[:half]
    dk_far_ref[...] = (dk_acc[half:] * SCALE).astype(jnp.bfloat16)
    dv_far_ref[...] = dv_acc[half:].astype(jnp.bfloat16)


SMEM_SPEC = pl.BlockSpec(memory_space=pltpu.SMEM)
VMEM_SPEC = pl.BlockSpec(memory_space=pltpu.VMEM)


def local_by_heads(
    query_heads,
    key_heads,
    value_heads,
    out_weight,
    cotangent,
    loss_mask,
    block_pattern,
    block_counts,
):
    tok_rows, local_cols = query_heads.shape
    head_count = local_cols // HD
    seq_devices = lax.axis_size("seq")
    own_blocks = head_count * tok_rows // BLK
    groups = [list(range(core, seq_devices, 2)) for core in range(2)]
    partner = [(source, source ^ 1) for source in range(seq_devices)]

    def exchanged(value):
        return lax.all_to_all(value, "seq", 0, 0, axis_index_groups=groups, tiled=True)

    def by_head(value):
        return jnp.transpose(value.reshape(tok_rows, head_count, HD), (1, 0, 2))

    def by_token(value):
        return jnp.transpose(value, (1, 0, 2)).reshape(tok_rows, local_cols)

    parity = (lax.axis_index("seq") % 2).astype(jnp.int32).reshape(1)
    masked = jnp.where(loss_mask[:, None] == 1, cotangent, jnp.zeros_like(cotangent))
    full_grad = lax.all_gather(masked, "tp", axis=1, tiled=True)

    keys_values = exchanged(jnp.stack([by_head(key_heads), by_head(value_heads)], axis=1))
    far = lax.ppermute(keys_values, "seq", partner)
    queries = exchanged(by_head(query_heads)).reshape(own_blocks, BLK, HD)
    keys = jnp.concatenate([keys_values[:, 0], far[:, 0]], 0).reshape(2 * own_blocks, BLK, HD)
    values = jnp.concatenate([keys_values[:, 1], far[:, 1]], 0).reshape(2 * own_blocks, BLK, HD)

    blocks_bf16 = jax.ShapeDtypeStruct((own_blocks, BLK, HD), jnp.bfloat16)
    blocks_f32 = jax.ShapeDtypeStruct((own_blocks, BLK, HD), jnp.float32)
    heads_blocks, log_total = pl.pallas_call(
        forward_kernel,
        out_shape=(blocks_bf16, jax.ShapeDtypeStruct((own_blocks, 1, BLK), jnp.float32)),
        in_specs=[SMEM_SPEC] * 3 + [VMEM_SPEC] * 3,
        out_specs=(VMEM_SPEC,) * 2,
        scratch_shapes=[pltpu.VMEM((block_pattern.shape[1], BLK, BLK), jnp.float32)],
        compiler_params=pltpu.CompilerParams(vmem_limit_bytes=VMEM_LIMIT),
        name="attention_forward",
    )(block_pattern, block_counts, parity, queries, keys, values)
    heads_out = by_token(exchanged(heads_blocks.reshape(head_count, tok_rows, HD)))

    d_heads = jnp.einsum(
        "td,cd->tc", full_grad, out_weight, preferred_element_type=jnp.float32
    ).astype(jnp.bfloat16)
    grads = exchanged(by_head(d_heads)).reshape(own_blocks, BLK, HD)

    partial_out = jnp.dot(heads_out, out_weight, preferred_element_type=jnp.float32)
    attended = lax.psum_scatter(
        partial_out.astype(jnp.bfloat16), "tp", scatter_dimension=1, tiled=True
    )
    weight_part = jnp.einsum("tc,td->cd", heads_out, full_grad, preferred_element_type=jnp.float32)
    weight_grad = lax.psum_scatter(
        weight_part.astype(jnp.bfloat16), "seq", scatter_dimension=1, tiled=True
    ).astype(jnp.float32)

    dq, dk, dv, dk_far, dv_far = pl.pallas_call(
        backward_kernel,
        out_shape=(blocks_bf16, blocks_f32, blocks_f32, blocks_bf16, blocks_bf16),
        in_specs=[SMEM_SPEC] * 3 + [VMEM_SPEC] * 6,
        out_specs=(VMEM_SPEC,) * 5,
        scratch_shapes=[pltpu.VMEM((2 * own_blocks, BLK, HD), jnp.float32)] * 2,
        compiler_params=pltpu.CompilerParams(vmem_limit_bytes=VMEM_LIMIT),
        name="attention_backward",
    )(block_pattern, block_counts, parity, queries, keys, values, heads_blocks, log_total, grads)
    dk_near, dv_near = lax.ppermute((dk_far, dv_far), "seq", partner)
    dk = (dk + dk_near.astype(jnp.float32)).astype(jnp.bfloat16)
    dv = (dv + dv_near.astype(jnp.float32)).astype(jnp.bfloat16)
    by_source = (head_count, tok_rows, HD)
    returned = exchanged(
        jnp.stack([dq.reshape(by_source), dk.reshape(by_source), dv.reshape(by_source)], axis=1)
    )
    query_grad, key_grad, value_grad = (by_token(returned[:, part]) for part in range(3))
    return (attended, query_grad, key_grad, value_grad, weight_grad)


def solution(mesh):
    in_specs = (
        P("seq", "tp"),
        P("seq", "tp"),
        P("seq", "tp"),
        P("tp", None),
        P("seq", "tp"),
        P("seq"),
        P(),
        P(),
    )
    out_specs = (P("seq", "tp"), P("seq", "tp"), P("seq", "tp"), P("seq", "tp"), P("tp", "seq"))

    def run(query_heads, *others):
        shard = (
            query_heads.shape[0] // mesh.shape["seq"],
            query_heads.shape[1] // mesh.shape["tp"],
        )
        one_head_a_chip = shard[0] == 2 * BLK and mesh.shape["seq"] == 2 * (shard[1] // HD)
        return jax.shard_map(
            local_by_heads if one_head_a_chip else local,
            mesh=mesh,
            in_specs=in_specs,
            out_specs=out_specs,
            check_vma=False,
        )(query_heads, *others)

    return run
```

```python
import functools
import math

import jax
import jax.numpy as jnp
from jax import lax
from jax.experimental import pallas as pl
from jax.experimental.pallas import tpu as pltpu
from jax.sharding import PartitionSpec as P

HD = 128
BLK = 256
WINDOW = 4


FLOOR_LOGIT = -1e30
SCALE = 1.0 / math.sqrt(HD)
LOG2_SCALE = SCALE * math.log2(math.e)
NT = (((1,), (1,)), ((), ()))
TN = (((0,), (0,)), ((), ()))
VMEM_LIMIT = 48 * 1024 * 1024


def passed_along(value, axis, steps):
    count = lax.axis_size(axis)
    leading, last = (max(0, -steps), min(count, count - steps))
    return lax.ppermute(value, axis, [(source, source + steps) for source in range(leading, last)])


def listed_table(block_pattern, block_counts, query_first, query_count, key_first, key_count):
    query_lists = lax.dynamic_slice_in_dim(block_pattern, query_first, query_count, 0)
    list_sizes = lax.dynamic_slice_in_dim(block_counts, query_first, query_count, 0)
    slot_ids = jnp.arange(block_pattern.shape[1], dtype=jnp.int32)
    in_use = slot_ids[None, :] < list_sizes[:, None]
    key_ids = key_first + jnp.arange(key_count, dtype=jnp.int32)
    matched = (query_lists[:, :, None] == key_ids[None, None, :]) & in_use[:, :, None]
    return jnp.any(matched, axis=1)


def masked_logits(query_part, key_part, listed):
    logits = jnp.einsum(
        "qhd,khd->hqk", query_part, key_part, preferred_element_type=jnp.float32
    ) * (1.0 / math.sqrt(HD))
    head_count, query_len, key_len = logits.shape
    blocked = logits.reshape(
        head_count,
        listed.shape[0],
        query_len // listed.shape[0],
        listed.shape[1],
        key_len // listed.shape[1],
    )
    blocked = jnp.where(listed[None, :, None, :, None], blocked, FLOOR_LOGIT)
    return blocked.reshape(head_count, query_len, key_len)


def piece_logits(query_part, key_part, listed):

    def compute(unused):
        return masked_logits(query_part, key_part, listed)

    def skipped(unused):
        return jnp.full(
            (query_part.shape[1], query_part.shape[0], key_part.shape[0]), FLOOR_LOGIT, jnp.float32
        )

    return lax.cond(jnp.any(listed), compute, skipped, 0)


def piece_output(logits, log_total, value_part, listed):

    def compute(unused):
        weights_b = jnp.exp(logits - log_total[:, :, None]).astype(jnp.bfloat16)
        return jnp.einsum("hqk,khd->hqd", weights_b, value_part, preferred_element_type=jnp.float32)

    def skipped(unused):
        return jnp.zeros((logits.shape[0], logits.shape[1], value_part.shape[2]), jnp.float32)

    return lax.cond(jnp.any(listed), compute, skipped, 0)


def pair_terms(
    logits,
    query_part,
    grad_part,
    log_total,
    row_dots,
    key_part,
    value_part,
    listed,
    want_query,
    want_keys,
):
    query_shape = query_part.shape
    key_shape = key_part.shape

    def compute(unused):
        scores = masked_logits(query_part, key_part, listed) if logits is None else logits
        weights = jnp.exp(scores - log_total[:, :, None])
        d_probs = jnp.einsum(
            "qhd,khd->hqk", grad_part, value_part, preferred_element_type=jnp.float32
        )
        d_logits = (weights * (d_probs - row_dots[:, :, None]) * (1.0 / math.sqrt(HD))).astype(
            jnp.bfloat16
        )
        query_term = jnp.zeros(query_shape, jnp.float32)
        key_term = jnp.zeros(key_shape, jnp.float32)
        value_term = jnp.zeros(key_shape, jnp.float32)
        if want_query:
            query_term = jnp.einsum(
                "hqk,khd->qhd", d_logits, key_part, preferred_element_type=jnp.float32
            )
        if want_keys:
            key_term = jnp.einsum(
                "hqk,qhd->khd", d_logits, query_part, preferred_element_type=jnp.float32
            )
            value_term = jnp.einsum(
                "hqk,qhd->khd",
                weights.astype(jnp.bfloat16),
                grad_part,
                preferred_element_type=jnp.float32,
            )
        return (query_term, key_term, value_term)

    def skipped(unused):
        return (
            jnp.zeros(query_shape, jnp.float32),
            jnp.zeros(key_shape, jnp.float32),
            jnp.zeros(key_shape, jnp.float32),
        )

    return lax.cond(jnp.any(listed), compute, skipped, 0)


def local(
    query_heads,
    key_heads,
    value_heads,
    out_weight,
    cotangent,
    loss_mask,
    block_pattern,
    block_counts,
):
    tok_rows = query_heads.shape[0]
    local_cols = query_heads.shape[1]
    head_count = local_cols // HD
    query_blocks = tok_rows // BLK
    seq_devices = lax.axis_size("seq")
    reach_dev = min((WINDOW * BLK + tok_rows - 1) // tok_rows, seq_devices - 1)
    position = lax.axis_index("seq")
    own_first = position * query_blocks
    query_part = query_heads.reshape(tok_rows, head_count, HD)
    offsets = [distance for distance in range(-reach_dev, reach_dev + 1) if distance != 0]
    neighbours = []
    for distance in offsets:
        arrived = passed_along((key_heads, value_heads), "seq", distance)
        neighbours.append((position - distance, arrived[0], arrived[1]))
    pieces = [(position, key_heads, value_heads)] + neighbours
    prepared = []
    for source, key_piece, value_piece in pieces:
        listed = listed_table(
            block_pattern,
            block_counts,
            own_first,
            query_blocks,
            source * query_blocks,
            query_blocks,
        )
        key_part = key_piece.reshape(tok_rows, head_count, HD)
        value_part = value_piece.reshape(tok_rows, head_count, HD)
        prepared.append((listed, key_part, value_part, piece_logits(query_part, key_part, listed)))
    highest = jnp.full((head_count, tok_rows), FLOOR_LOGIT, jnp.float32)
    for listed, key_part, value_part, logits in prepared:
        highest = jnp.maximum(highest, jnp.max(logits, axis=2))
    denominator = jnp.zeros((head_count, tok_rows), jnp.float32)
    for listed, key_part, value_part, logits in prepared:
        denominator = denominator + jnp.sum(jnp.exp(logits - highest[:, :, None]), axis=2)
    log_total = highest + jnp.log(denominator)
    weighted = jnp.zeros((head_count, tok_rows, HD), jnp.float32)
    for listed, key_part, value_part, logits in prepared:
        weighted = weighted + piece_output(logits, log_total, value_part, listed)
    heads_out = (
        jnp.transpose(weighted, (1, 0, 2)).reshape(tok_rows, local_cols).astype(jnp.bfloat16)
    )
    partial_out = jnp.dot(heads_out, out_weight, preferred_element_type=jnp.float32)
    attended = lax.psum_scatter(partial_out, "tp", scatter_dimension=1, tiled=True).astype(
        jnp.bfloat16
    )
    masked = jnp.where(loss_mask[:, None] == 1, cotangent, jnp.zeros_like(cotangent))
    full_grad = lax.all_gather(masked, "tp", axis=1, tiled=True)
    weight_part = jnp.einsum("tc,td->cd", heads_out, full_grad, preferred_element_type=jnp.float32)
    weight_grad = lax.psum_scatter(weight_part, "seq", scatter_dimension=1, tiled=True)
    d_heads = jnp.einsum(
        "td,cd->tc", full_grad, out_weight, preferred_element_type=jnp.float32
    ).astype(jnp.bfloat16)
    grad_part = d_heads.reshape(tok_rows, head_count, HD)
    row_dots = jnp.sum(
        grad_part.astype(jnp.float32)
        * heads_out.reshape(tok_rows, head_count, HD).astype(jnp.float32),
        axis=2,
    ).T
    own_listed, own_keys, own_values, own_logits = prepared[0]
    term_set = pair_terms(
        own_logits,
        query_part,
        grad_part,
        log_total,
        row_dots,
        own_keys,
        own_values,
        own_listed,
        True,
        True,
    )
    query_acc, key_acc, value_acc = term_set
    for listed, key_part, value_part, logits in prepared[1:]:
        term_set = pair_terms(
            logits,
            query_part,
            grad_part,
            log_total,
            row_dots,
            key_part,
            value_part,
            listed,
            True,
            False,
        )
        query_acc = query_acc + term_set[0]
    for distance in offsets:
        arrived = passed_along((query_heads, d_heads), "seq", distance)
        arrived_stats = passed_along((log_total, row_dots), "seq", distance)
        sender = position - distance
        inside = (sender >= 0) & (sender < seq_devices)
        listed = (
            listed_table(
                block_pattern,
                block_counts,
                sender * query_blocks,
                query_blocks,
                own_first,
                query_blocks,
            )
            & inside
        )
        term_set = pair_terms(
            None,
            arrived[0].reshape(tok_rows, head_count, HD),
            arrived[1].reshape(tok_rows, head_count, HD),
            arrived_stats[0],
            arrived_stats[1],
            own_keys,
            own_values,
            listed,
            False,
            True,
        )
        key_acc = key_acc + term_set[1]
        value_acc = value_acc + term_set[2]
    query_grad = query_acc.reshape(tok_rows, local_cols).astype(jnp.bfloat16)
    key_grad = key_acc.reshape(tok_rows, local_cols).astype(jnp.bfloat16)
    value_grad = value_acc.reshape(tok_rows, local_cols).astype(jnp.bfloat16)
    return (attended, query_grad, key_grad, value_grad, weight_grad)


def block_slot(block, parity):
    return (((block // 2) + parity) % 2) * 8 + (block // 4) * 2 + block % 2


def forward_kernel(pattern, counts, parity_ref, q_ref, k_ref, v_ref, out_ref, total_ref, scores):
    parity = parity_ref[0]

    def query_block(index, carry):
        block = 4 * (index // 2) + 2 * parity + index % 2
        entries = counts[block]
        query = q_ref[index]

        def score(entry, highest):
            slot = block_slot(pattern[block, entry], parity)
            logits = (
                lax.dot_general(k_ref[slot], query, NT, preferred_element_type=jnp.float32)
                * LOG2_SCALE
            )
            scores[entry] = logits
            return jnp.maximum(highest, jnp.max(logits, axis=0, keepdims=True))

        highest = lax.fori_loop(0, entries, score, jnp.full((1, BLK), FLOOR_LOGIT, jnp.float32))

        def blend(entry, state):
            total, mixed = state
            slot = block_slot(pattern[block, entry], parity)
            weights = jnp.exp2(scores[entry] - highest)
            total = total + jnp.sum(weights, axis=0, keepdims=True)
            mixed = mixed + lax.dot_general(
                v_ref[slot], weights.astype(jnp.bfloat16), TN, preferred_element_type=jnp.float32
            )
            return total, mixed

        total, mixed = lax.fori_loop(
            0,
            entries,
            blend,
            (jnp.zeros((1, BLK), jnp.float32), jnp.zeros((HD, BLK), jnp.float32)),
        )
        out_ref[index] = jnp.transpose(mixed / total).astype(jnp.bfloat16)
        total_ref[index] = highest + jnp.log2(total)
        return carry

    lax.fori_loop(0, q_ref.shape[0], query_block, 0)


def backward_kernel(
    pattern,
    counts,
    parity_ref,
    q_ref,
    k_ref,
    v_ref,
    out_ref,
    total_ref,
    grad_ref,
    dq_ref,
    dk_ref,
    dv_ref,
    dk_far_ref,
    dv_far_ref,
    dk_acc,
    dv_acc,
):
    parity = parity_ref[0]
    dk_acc[...] = jnp.zeros_like(dk_acc)
    dv_acc[...] = jnp.zeros_like(dv_acc)

    def query_block(index, carry):
        block = 4 * (index // 2) + 2 * parity + index % 2
        query = q_ref[index]
        grad = grad_ref[index]
        log_total = total_ref[index]
        products = grad.astype(jnp.float32) * out_ref[index].astype(jnp.float32)
        row_dots = jnp.sum(jnp.transpose(products), axis=0, keepdims=True)

        def pair(entry, dq):
            slot = block_slot(pattern[block, entry], parity)
            key = k_ref[slot]
            logits = (
                lax.dot_general(key, query, NT, preferred_element_type=jnp.float32) * LOG2_SCALE
            )
            weights = jnp.exp2(logits - log_total)
            d_probs = lax.dot_general(v_ref[slot], grad, NT, preferred_element_type=jnp.float32)
            d_logits = (weights * (d_probs - row_dots)).astype(jnp.bfloat16)
            dv_acc[slot] += jnp.dot(
                weights.astype(jnp.bfloat16), grad, preferred_element_type=jnp.float32
            )
            dk_acc[slot] += jnp.dot(d_logits, query, preferred_element_type=jnp.float32)
            return dq + lax.dot_general(key, d_logits, TN, preferred_element_type=jnp.float32)

        dq = lax.fori_loop(0, counts[block], pair, jnp.zeros((HD, BLK), jnp.float32))
        dq_ref[index] = jnp.transpose(dq * SCALE).astype(jnp.bfloat16)
        return carry

    lax.fori_loop(0, q_ref.shape[0], query_block, 0)
    half = dk_acc.shape[0] // 2
    dk_ref[...] = dk_acc[:half] * SCALE
    dv_ref[...] = dv_acc[:half]
    dk_far_ref[...] = (dk_acc[half:] * SCALE).astype(jnp.bfloat16)
    dv_far_ref[...] = dv_acc[half:].astype(jnp.bfloat16)


SMEM_SPEC = pl.BlockSpec(memory_space=pltpu.SMEM)
VMEM_SPEC = pl.BlockSpec(memory_space=pltpu.VMEM)
ANY_SPEC = pl.BlockSpec(memory_space=pl.ANY)


def chip_peers():
    place = lax.axis_index("seq")
    chip, core = place // 2, place % 2
    others = (chip + 1 - 2 * (chip % 2), (chip + 2) % 4, 3 - chip)
    return chip, core, [(other, 2 * other + core) for other in others]


def meet(devices):
    barrier = pltpu.get_barrier_semaphore()
    for device in devices:
        pl.semaphore_signal(
            barrier, inc=1, device_id={"seq": device}, device_id_type=pl.DeviceIdType.MESH
        )
    pl.semaphore_wait(barrier, len(devices))


def remote(source, target, send_sem, recv_sem, device):
    return pltpu.make_async_remote_copy(
        src_ref=source,
        dst_ref=target,
        send_sem=send_sem,
        recv_sem=recv_sem,
        device_id={"seq": device},
        device_id_type=pl.DeviceIdType.MESH,
    )


def head_columns(head):
    return pl.ds(pl.multiple_of(head * HD, HD), HD)


def spread_kernel(shared, count, *refs):
    sources, targets = refs[:count], refs[count : 2 * count]
    own_sem, send_sem, recv_sem, pass_sem, passed_sem = refs[2 * count :]
    chip, core, peers = chip_peers()
    partner = 2 * chip + 1 - core
    meet([device for _, device in peers] + ([partner] if shared else []))
    sent, kept, passed = [], [], []
    for a in range(count):
        for k, (other, device) in enumerate(peers):
            sent.append(
                remote(
                    sources[a].at[:, head_columns(other)],
                    targets[a].at[chip],
                    send_sem.at[a, k],
                    recv_sem.at[a, k],
                    device,
                )
            )
            sent[-1].start()
        kept.append(
            pltpu.make_async_copy(
                sources[a].at[:, head_columns(chip)], targets[a].at[chip], own_sem.at[a]
            )
        )
        kept[-1].start()
        if a < shared:
            passed.append(
                remote(
                    sources[a].at[:, head_columns(chip)],
                    targets[a].at[4 + chip],
                    pass_sem.at[a, 3],
                    passed_sem.at[a, 3],
                    partner,
                )
            )
            passed[-1].start()
    for a in range(count):
        for k, (other, device) in enumerate(peers):
            sent[3 * a + k].wait_recv()
            if a < shared:
                passed.append(
                    remote(
                        targets[a].at[other],
                        targets[a].at[4 + other],
                        pass_sem.at[a, k],
                        passed_sem.at[a, k],
                        partner,
                    )
                )
                passed[-1].start()
    for copy in kept:
        copy.wait()
    for copy in sent:
        copy.wait_send()
    for copy in passed:
        copy.wait()


def spread(arrays, shared, collective_id):
    count = len(arrays)
    rows, columns = arrays[0].shape
    heads = columns // HD
    slots = [2 * heads if a < shared else heads for a in range(count)]
    return pl.pallas_call(
        functools.partial(spread_kernel, shared, count),
        out_shape=tuple(jax.ShapeDtypeStruct((n, rows, HD), jnp.bfloat16) for n in slots),
        in_specs=[ANY_SPEC] * count,
        out_specs=(ANY_SPEC,) * count,
        scratch_shapes=[
            pltpu.SemaphoreType.DMA((count,)),
            pltpu.SemaphoreType.DMA((count, 3)),
            pltpu.SemaphoreType.DMA((count, 3)),
            pltpu.SemaphoreType.DMA((count, 4)),
            pltpu.SemaphoreType.DMA((count, 4)),
        ],
        compiler_params=pltpu.CompilerParams(collective_id=collective_id, has_side_effects=True),
        name="spread_heads",
    )(*arrays)


def collect_kernel(source, target, own_sem, send_sem, recv_sem):
    chip, core, peers = chip_peers()
    meet([device for _, device in peers])
    copies = []
    for k, (other, device) in enumerate(peers):
        copies.append(
            remote(
                source.at[other],
                target.at[:, head_columns(chip)],
                send_sem.at[k],
                recv_sem.at[k],
                device,
            )
        )
    copies.append(
        pltpu.make_async_copy(source.at[chip], target.at[:, head_columns(chip)], own_sem)
    )
    for copy in copies:
        copy.start()
    for copy in copies:
        copy.wait()


def collect(array, collective_id):
    heads, rows, _ = array.shape
    return pl.pallas_call(
        collect_kernel,
        out_shape=jax.ShapeDtypeStruct((rows, heads * HD), jnp.bfloat16),
        in_specs=[ANY_SPEC],
        out_specs=ANY_SPEC,
        scratch_shapes=[
            pltpu.SemaphoreType.DMA,
            pltpu.SemaphoreType.DMA((3,)),
            pltpu.SemaphoreType.DMA((3,)),
        ],
        compiler_params=pltpu.CompilerParams(collective_id=collective_id, has_side_effects=True),
        name="collect_heads",
    )(array)


def collect_grads_kernel(
    dq_ref,
    dk_ref,
    dv_ref,
    dk_far_ref,
    dv_far_ref,
    query_grad,
    key_grad,
    value_grad,
    near,
    summed,
    pass_sem,
    passed_sem,
    own_sem,
    send_sem,
    recv_sem,
):
    chip, core, peers = chip_peers()
    partner = 2 * chip + 1 - core
    meet([device for _, device in peers] + [partner])
    order = [(k, other, device) for k, (other, device) in enumerate(peers)] + [(3, chip, None)]
    passed, copies = [], []
    for k, other, _ in order:
        for a, far in enumerate((dk_far_ref, dv_far_ref)):
            passed.append(
                remote(
                    far.at[other], near.at[a, other], pass_sem.at[a, k], passed_sem.at[a, k], partner
                )
            )
            passed[-1].start()

    def send(a, source, target, k, other, device):
        place = target.at[:, head_columns(chip)]
        if device is None:
            copies.append(pltpu.make_async_copy(source, place, own_sem.at[a]))
        else:
            copies.append(remote(source, place, send_sem.at[a, k], recv_sem.at[a, k], device))
        copies[-1].start()

    for k, other, device in order:
        send(2, dq_ref.at[other], query_grad, k, other, device)
    for k, other, device in order:
        for a, (share, target) in enumerate(((dk_ref, key_grad), (dv_ref, value_grad))):
            passed[2 * k + a].wait_recv()
            summed[a, other] = (share[other] + near[a, other].astype(jnp.float32)).astype(
                jnp.bfloat16
            )
            send(a, summed.at[a, other], target, k, other, device)
    for copy in passed:
        copy.wait_send()
    for copy in copies:
        copy.wait()


def collect_grads(dq, dk, dv, dk_far, dv_far, collective_id):
    heads, rows, _ = dq.shape
    return pl.pallas_call(
        collect_grads_kernel,
        out_shape=(jax.ShapeDtypeStruct((rows, heads * HD), jnp.bfloat16),) * 3,
        in_specs=[ANY_SPEC, VMEM_SPEC, VMEM_SPEC, ANY_SPEC, ANY_SPEC],
        out_specs=(ANY_SPEC,) * 3,
        scratch_shapes=[
            pltpu.VMEM((2, heads, rows, HD), jnp.bfloat16),
            pltpu.VMEM((2, heads, rows, HD), jnp.bfloat16),
            pltpu.SemaphoreType.DMA((2, 4)),
            pltpu.SemaphoreType.DMA((2, 4)),
            pltpu.SemaphoreType.DMA((3,)),
            pltpu.SemaphoreType.DMA((3, 3)),
            pltpu.SemaphoreType.DMA((3, 3)),
        ],
        compiler_params=pltpu.CompilerParams(
            collective_id=collective_id, has_side_effects=True, vmem_limit_bytes=VMEM_LIMIT
        ),
        name="collect_grads",
    )(dq, dk, dv, dk_far, dv_far)


def summed_over_plane(heads_out, full_grad):
    rows, width = full_grad.shape
    seq_devices = lax.axis_size("seq")
    chips = seq_devices // 2
    place = lax.axis_index("seq")
    chip, core = place // 2, place % 2
    chunks = full_grad.reshape(rows, chips, 2, width // seq_devices)

    def share(which):
        columns = lax.dynamic_index_in_dim(chunks, which, 2, keepdims=False)
        return jnp.einsum("tc,tkd->kcd", heads_out, columns, preferred_element_type=jnp.float32)

    far = lax.ppermute(
        share(1 - core).astype(jnp.bfloat16),
        "seq",
        [(source, source ^ 1) for source in range(seq_devices)],
    )
    both = share(core) + far.astype(jnp.float32)
    total = lax.dynamic_index_in_dim(both, chip, 0, keepdims=False)
    for step in range(1, chips):
        piece = lax.dynamic_index_in_dim(both, chip ^ step, 0, keepdims=False)
        arrived = lax.ppermute(
            piece.astype(jnp.bfloat16),
            "seq",
            [(source, source ^ (2 * step)) for source in range(seq_devices)],
        )
        total = total + arrived.astype(jnp.float32)
    return total


def local_by_heads(
    query_heads,
    key_heads,
    value_heads,
    out_weight,
    cotangent,
    loss_mask,
    block_pattern,
    block_counts,
):
    tok_rows, local_cols = query_heads.shape
    head_count = local_cols // HD
    own_blocks = head_count * tok_rows // BLK
    parity = (lax.axis_index("seq") % 2).astype(jnp.int32).reshape(1)
    masked = jnp.where(loss_mask[:, None] == 1, cotangent, jnp.zeros_like(cotangent))
    full_grad = lax.all_gather(masked, "tp", axis=1, tiled=True)

    keys, values, queries = spread((key_heads, value_heads, query_heads), 2, 0)
    keys = keys.reshape(2 * own_blocks, BLK, HD)
    values = values.reshape(2 * own_blocks, BLK, HD)
    queries = queries.reshape(own_blocks, BLK, HD)

    blocks_bf16 = jax.ShapeDtypeStruct((own_blocks, BLK, HD), jnp.bfloat16)
    blocks_f32 = jax.ShapeDtypeStruct((own_blocks, BLK, HD), jnp.float32)
    heads_blocks, log_total = pl.pallas_call(
        forward_kernel,
        out_shape=(blocks_bf16, jax.ShapeDtypeStruct((own_blocks, 1, BLK), jnp.float32)),
        in_specs=[SMEM_SPEC] * 3 + [VMEM_SPEC] * 3,
        out_specs=(VMEM_SPEC,) * 2,
        scratch_shapes=[pltpu.VMEM((block_pattern.shape[1], BLK, BLK), jnp.float32)],
        compiler_params=pltpu.CompilerParams(vmem_limit_bytes=VMEM_LIMIT),
        name="attention_forward",
    )(block_pattern, block_counts, parity, queries, keys, values)
    heads_out = collect(heads_blocks.reshape(head_count, tok_rows, HD), 1)

    d_heads = jnp.einsum(
        "td,cd->tc", full_grad, out_weight, preferred_element_type=jnp.float32
    ).astype(jnp.bfloat16)
    (grads,) = spread((d_heads,), 0, 2)
    grads = grads.reshape(own_blocks, BLK, HD)

    partial_out = jnp.dot(heads_out, out_weight, preferred_element_type=jnp.float32)
    attended = lax.psum_scatter(
        partial_out.astype(jnp.bfloat16), "tp", scatter_dimension=1, tiled=True
    )
    weight_grad = summed_over_plane(heads_out, full_grad)

    dq, dk, dv, dk_far, dv_far = pl.pallas_call(
        backward_kernel,
        out_shape=(blocks_bf16, blocks_f32, blocks_f32, blocks_bf16, blocks_bf16),
        in_specs=[SMEM_SPEC] * 3 + [VMEM_SPEC] * 6,
        out_specs=(VMEM_SPEC,) * 5,
        scratch_shapes=[pltpu.VMEM((2 * own_blocks, BLK, HD), jnp.float32)] * 2,
        compiler_params=pltpu.CompilerParams(vmem_limit_bytes=VMEM_LIMIT),
        name="attention_backward",
    )(block_pattern, block_counts, parity, queries, keys, values, heads_blocks, log_total, grads)
    by_source = (head_count, tok_rows, HD)
    query_grad, key_grad, value_grad = collect_grads(
        *(part.reshape(by_source) for part in (dq, dk, dv, dk_far, dv_far)), 3
    )
    return (attended, query_grad, key_grad, value_grad, weight_grad)


def solution(mesh):
    in_specs = (
        P("seq", "tp"),
        P("seq", "tp"),
        P("seq", "tp"),
        P("tp", None),
        P("seq", "tp"),
        P("seq"),
        P(),
        P(),
    )
    out_specs = (P("seq", "tp"), P("seq", "tp"), P("seq", "tp"), P("seq", "tp"), P("tp", "seq"))

    def run(query_heads, *others):
        shard = (
            query_heads.shape[0] // mesh.shape["seq"],
            query_heads.shape[1] // mesh.shape["tp"],
        )
        one_head_a_chip = shard[0] == 2 * BLK and mesh.shape["seq"] == 2 * (shard[1] // HD)
        return jax.shard_map(
            local_by_heads if one_head_a_chip else local,
            mesh=mesh,
            in_specs=in_specs,
            out_specs=out_specs,
            check_vma=False,
        )(query_heads, *others)

    return run
```

```python
import functools
import math

import jax
import jax.numpy as jnp
from jax import lax
from jax.experimental import pallas as pl
from jax.experimental.pallas import tpu as pltpu
from jax.sharding import PartitionSpec as P

HD = 128
BLK = 256
WINDOW = 4


FLOOR_LOGIT = -1e30
SCALE = 1.0 / math.sqrt(HD)
LOG2_SCALE = SCALE * math.log2(math.e)
NT = (((1,), (1,)), ((), ()))
TN = (((0,), (0,)), ((), ()))
VMEM_LIMIT = 48 * 1024 * 1024


def passed_along(value, axis, steps):
    count = lax.axis_size(axis)
    leading, last = (max(0, -steps), min(count, count - steps))
    return lax.ppermute(value, axis, [(source, source + steps) for source in range(leading, last)])


def listed_table(block_pattern, block_counts, query_first, query_count, key_first, key_count):
    query_lists = lax.dynamic_slice_in_dim(block_pattern, query_first, query_count, 0)
    list_sizes = lax.dynamic_slice_in_dim(block_counts, query_first, query_count, 0)
    slot_ids = jnp.arange(block_pattern.shape[1], dtype=jnp.int32)
    in_use = slot_ids[None, :] < list_sizes[:, None]
    key_ids = key_first + jnp.arange(key_count, dtype=jnp.int32)
    matched = (query_lists[:, :, None] == key_ids[None, None, :]) & in_use[:, :, None]
    return jnp.any(matched, axis=1)


def masked_logits(query_part, key_part, listed):
    logits = jnp.einsum(
        "qhd,khd->hqk", query_part, key_part, preferred_element_type=jnp.float32
    ) * (1.0 / math.sqrt(HD))
    head_count, query_len, key_len = logits.shape
    blocked = logits.reshape(
        head_count,
        listed.shape[0],
        query_len // listed.shape[0],
        listed.shape[1],
        key_len // listed.shape[1],
    )
    blocked = jnp.where(listed[None, :, None, :, None], blocked, FLOOR_LOGIT)
    return blocked.reshape(head_count, query_len, key_len)


def piece_logits(query_part, key_part, listed):

    def compute(unused):
        return masked_logits(query_part, key_part, listed)

    def skipped(unused):
        return jnp.full(
            (query_part.shape[1], query_part.shape[0], key_part.shape[0]), FLOOR_LOGIT, jnp.float32
        )

    return lax.cond(jnp.any(listed), compute, skipped, 0)


def piece_output(logits, log_total, value_part, listed):

    def compute(unused):
        weights_b = jnp.exp(logits - log_total[:, :, None]).astype(jnp.bfloat16)
        return jnp.einsum("hqk,khd->hqd", weights_b, value_part, preferred_element_type=jnp.float32)

    def skipped(unused):
        return jnp.zeros((logits.shape[0], logits.shape[1], value_part.shape[2]), jnp.float32)

    return lax.cond(jnp.any(listed), compute, skipped, 0)


def pair_terms(
    logits,
    query_part,
    grad_part,
    log_total,
    row_dots,
    key_part,
    value_part,
    listed,
    want_query,
    want_keys,
):
    query_shape = query_part.shape
    key_shape = key_part.shape

    def compute(unused):
        scores = masked_logits(query_part, key_part, listed) if logits is None else logits
        weights = jnp.exp(scores - log_total[:, :, None])
        d_probs = jnp.einsum(
            "qhd,khd->hqk", grad_part, value_part, preferred_element_type=jnp.float32
        )
        d_logits = (weights * (d_probs - row_dots[:, :, None]) * (1.0 / math.sqrt(HD))).astype(
            jnp.bfloat16
        )
        query_term = jnp.zeros(query_shape, jnp.float32)
        key_term = jnp.zeros(key_shape, jnp.float32)
        value_term = jnp.zeros(key_shape, jnp.float32)
        if want_query:
            query_term = jnp.einsum(
                "hqk,khd->qhd", d_logits, key_part, preferred_element_type=jnp.float32
            )
        if want_keys:
            key_term = jnp.einsum(
                "hqk,qhd->khd", d_logits, query_part, preferred_element_type=jnp.float32
            )
            value_term = jnp.einsum(
                "hqk,qhd->khd",
                weights.astype(jnp.bfloat16),
                grad_part,
                preferred_element_type=jnp.float32,
            )
        return (query_term, key_term, value_term)

    def skipped(unused):
        return (
            jnp.zeros(query_shape, jnp.float32),
            jnp.zeros(key_shape, jnp.float32),
            jnp.zeros(key_shape, jnp.float32),
        )

    return lax.cond(jnp.any(listed), compute, skipped, 0)


def local(
    query_heads,
    key_heads,
    value_heads,
    out_weight,
    cotangent,
    loss_mask,
    block_pattern,
    block_counts,
):
    tok_rows = query_heads.shape[0]
    local_cols = query_heads.shape[1]
    head_count = local_cols // HD
    query_blocks = tok_rows // BLK
    seq_devices = lax.axis_size("seq")
    reach_dev = min((WINDOW * BLK + tok_rows - 1) // tok_rows, seq_devices - 1)
    position = lax.axis_index("seq")
    own_first = position * query_blocks
    query_part = query_heads.reshape(tok_rows, head_count, HD)
    offsets = [distance for distance in range(-reach_dev, reach_dev + 1) if distance != 0]
    neighbours = []
    for distance in offsets:
        arrived = passed_along((key_heads, value_heads), "seq", distance)
        neighbours.append((position - distance, arrived[0], arrived[1]))
    pieces = [(position, key_heads, value_heads)] + neighbours
    prepared = []
    for source, key_piece, value_piece in pieces:
        listed = listed_table(
            block_pattern,
            block_counts,
            own_first,
            query_blocks,
            source * query_blocks,
            query_blocks,
        )
        key_part = key_piece.reshape(tok_rows, head_count, HD)
        value_part = value_piece.reshape(tok_rows, head_count, HD)
        prepared.append((listed, key_part, value_part, piece_logits(query_part, key_part, listed)))
    highest = jnp.full((head_count, tok_rows), FLOOR_LOGIT, jnp.float32)
    for listed, key_part, value_part, logits in prepared:
        highest = jnp.maximum(highest, jnp.max(logits, axis=2))
    denominator = jnp.zeros((head_count, tok_rows), jnp.float32)
    for listed, key_part, value_part, logits in prepared:
        denominator = denominator + jnp.sum(jnp.exp(logits - highest[:, :, None]), axis=2)
    log_total = highest + jnp.log(denominator)
    weighted = jnp.zeros((head_count, tok_rows, HD), jnp.float32)
    for listed, key_part, value_part, logits in prepared:
        weighted = weighted + piece_output(logits, log_total, value_part, listed)
    heads_out = (
        jnp.transpose(weighted, (1, 0, 2)).reshape(tok_rows, local_cols).astype(jnp.bfloat16)
    )
    partial_out = jnp.dot(heads_out, out_weight, preferred_element_type=jnp.float32)
    attended = lax.psum_scatter(partial_out, "tp", scatter_dimension=1, tiled=True).astype(
        jnp.bfloat16
    )
    masked = jnp.where(loss_mask[:, None] == 1, cotangent, jnp.zeros_like(cotangent))
    full_grad = lax.all_gather(masked, "tp", axis=1, tiled=True)
    weight_part = jnp.einsum("tc,td->cd", heads_out, full_grad, preferred_element_type=jnp.float32)
    weight_grad = lax.psum_scatter(weight_part, "seq", scatter_dimension=1, tiled=True)
    d_heads = jnp.einsum(
        "td,cd->tc", full_grad, out_weight, preferred_element_type=jnp.float32
    ).astype(jnp.bfloat16)
    grad_part = d_heads.reshape(tok_rows, head_count, HD)
    row_dots = jnp.sum(
        grad_part.astype(jnp.float32)
        * heads_out.reshape(tok_rows, head_count, HD).astype(jnp.float32),
        axis=2,
    ).T
    own_listed, own_keys, own_values, own_logits = prepared[0]
    term_set = pair_terms(
        own_logits,
        query_part,
        grad_part,
        log_total,
        row_dots,
        own_keys,
        own_values,
        own_listed,
        True,
        True,
    )
    query_acc, key_acc, value_acc = term_set
    for listed, key_part, value_part, logits in prepared[1:]:
        term_set = pair_terms(
            logits,
            query_part,
            grad_part,
            log_total,
            row_dots,
            key_part,
            value_part,
            listed,
            True,
            False,
        )
        query_acc = query_acc + term_set[0]
    for distance in offsets:
        arrived = passed_along((query_heads, d_heads), "seq", distance)
        arrived_stats = passed_along((log_total, row_dots), "seq", distance)
        sender = position - distance
        inside = (sender >= 0) & (sender < seq_devices)
        listed = (
            listed_table(
                block_pattern,
                block_counts,
                sender * query_blocks,
                query_blocks,
                own_first,
                query_blocks,
            )
            & inside
        )
        term_set = pair_terms(
            None,
            arrived[0].reshape(tok_rows, head_count, HD),
            arrived[1].reshape(tok_rows, head_count, HD),
            arrived_stats[0],
            arrived_stats[1],
            own_keys,
            own_values,
            listed,
            False,
            True,
        )
        key_acc = key_acc + term_set[1]
        value_acc = value_acc + term_set[2]
    query_grad = query_acc.reshape(tok_rows, local_cols).astype(jnp.bfloat16)
    key_grad = key_acc.reshape(tok_rows, local_cols).astype(jnp.bfloat16)
    value_grad = value_acc.reshape(tok_rows, local_cols).astype(jnp.bfloat16)
    return (attended, query_grad, key_grad, value_grad, weight_grad)


def block_slot(block, parity):
    return (((block // 2) + parity) % 2) * 8 + (block // 4) * 2 + block % 2


def entry_pair(step, entries):
    first = 2 * step
    second = jnp.minimum(first + 1, entries - 1)
    return (first, 0.0), (second, jnp.where(first + 1 < entries, 0.0, -FLOOR_LOGIT))


def forward_kernel(pattern, counts, parity_ref, q_ref, k_ref, v_ref, out_ref, total_ref, scores):
    parity = parity_ref[0]

    def query_block(index, carry):
        block = 4 * (index // 2) + 2 * parity + index % 2
        entries = counts[block]
        query = q_ref[index]

        steps = (entries + 1) // 2

        def score(step, highest):
            for entry, _ in entry_pair(step, entries):
                slot = block_slot(pattern[block, entry], parity)
                logits = (
                    lax.dot_general(k_ref[slot], query, NT, preferred_element_type=jnp.float32)
                    * LOG2_SCALE
                )
                scores[entry] = logits
                highest = jnp.maximum(highest, jnp.max(logits, axis=0, keepdims=True))
            return highest

        highest = lax.fori_loop(0, steps, score, jnp.full((1, BLK), FLOOR_LOGIT, jnp.float32))

        def blend(step, state):
            total, mixed = state
            for entry, penalty in entry_pair(step, entries):
                slot = block_slot(pattern[block, entry], parity)
                weights = jnp.exp2(scores[entry] - (highest + penalty))
                total = total + jnp.sum(weights, axis=0, keepdims=True)
                mixed = mixed + lax.dot_general(
                    v_ref[slot],
                    weights.astype(jnp.bfloat16),
                    TN,
                    preferred_element_type=jnp.float32,
                )
            return total, mixed

        total, mixed = lax.fori_loop(
            0,
            steps,
            blend,
            (jnp.zeros((1, BLK), jnp.float32), jnp.zeros((HD, BLK), jnp.float32)),
        )
        out_ref[index] = jnp.transpose(mixed / total).astype(jnp.bfloat16)
        total_ref[index] = highest + jnp.log2(total)
        return carry

    lax.fori_loop(0, q_ref.shape[0], query_block, 0)


def backward_kernel(
    pattern,
    counts,
    parity_ref,
    q_ref,
    k_ref,
    v_ref,
    out_ref,
    total_ref,
    grad_ref,
    dq_ref,
    dk_ref,
    dv_ref,
    dk_far_ref,
    dv_far_ref,
    dk_acc,
    dv_acc,
):
    parity = parity_ref[0]
    dk_acc[...] = jnp.zeros_like(dk_acc)
    dv_acc[...] = jnp.zeros_like(dv_acc)

    def query_block(index, carry):
        block = 4 * (index // 2) + 2 * parity + index % 2
        query = q_ref[index]
        grad = grad_ref[index]
        log_total = total_ref[index]
        products = grad.astype(jnp.float32) * out_ref[index].astype(jnp.float32)
        row_dots = jnp.sum(jnp.transpose(products), axis=0, keepdims=True)

        entries = counts[block]

        def pair(step, dq):
            for entry, penalty in entry_pair(step, entries):
                slot = block_slot(pattern[block, entry], parity)
                key = k_ref[slot]
                logits = (
                    lax.dot_general(key, query, NT, preferred_element_type=jnp.float32) * LOG2_SCALE
                )
                weights = jnp.exp2(logits - (log_total + penalty))
                d_probs = lax.dot_general(
                    v_ref[slot], grad, NT, preferred_element_type=jnp.float32
                )
                d_logits = (weights * (d_probs - row_dots)).astype(jnp.bfloat16)
                dv_acc[slot] += jnp.dot(
                    weights.astype(jnp.bfloat16), grad, preferred_element_type=jnp.float32
                )
                dk_acc[slot] += jnp.dot(d_logits, query, preferred_element_type=jnp.float32)
                dq = dq + lax.dot_general(key, d_logits, TN, preferred_element_type=jnp.float32)
            return dq

        dq = lax.fori_loop(0, (entries + 1) // 2, pair, jnp.zeros((HD, BLK), jnp.float32))
        dq_ref[index] = jnp.transpose(dq * SCALE).astype(jnp.bfloat16)
        return carry

    lax.fori_loop(0, q_ref.shape[0], query_block, 0)
    half = dk_acc.shape[0] // 2
    dk_ref[...] = dk_acc[:half] * SCALE
    dv_ref[...] = dv_acc[:half]
    dk_far_ref[...] = (dk_acc[half:] * SCALE).astype(jnp.bfloat16)
    dv_far_ref[...] = dv_acc[half:].astype(jnp.bfloat16)


def cost(microseconds):
    return pl.CostEstimate(
        flops=microseconds * 10**9, bytes_accessed=microseconds * 3 * 10**6, transcendentals=0
    )


SMEM_SPEC = pl.BlockSpec(memory_space=pltpu.SMEM)
VMEM_SPEC = pl.BlockSpec(memory_space=pltpu.VMEM)
ANY_SPEC = pl.BlockSpec(memory_space=pl.ANY)


def chip_peers():
    place = lax.axis_index("seq")
    chip, core = place // 2, place % 2
    others = (chip + 1 - 2 * (chip % 2), (chip + 2) % 4, 3 - chip)
    return chip, core, [(other, 2 * other + core) for other in others]


def meet(devices):
    barrier = pltpu.get_barrier_semaphore()
    for device in devices:
        pl.semaphore_signal(
            barrier, inc=1, device_id={"seq": device}, device_id_type=pl.DeviceIdType.MESH
        )
    pl.semaphore_wait(barrier, len(devices))


def remote(source, target, send_sem, recv_sem, device):
    return pltpu.make_async_remote_copy(
        src_ref=source,
        dst_ref=target,
        send_sem=send_sem,
        recv_sem=recv_sem,
        device_id={"seq": device},
        device_id_type=pl.DeviceIdType.MESH,
    )


def head_columns(head):
    return pl.ds(pl.multiple_of(head * HD, HD), HD)


def spread_kernel(shared, count, *refs):
    sources, targets = refs[:count], refs[count : 2 * count]
    own_sem, send_sem, recv_sem, pass_sem, passed_sem = refs[2 * count :]
    chip, core, peers = chip_peers()
    partner = 2 * chip + 1 - core
    meet([device for _, device in peers] + ([partner] if shared else []))
    sent, kept, passed = [], [], []
    for a in range(count):
        for k, (other, device) in enumerate(peers):
            sent.append(
                remote(
                    sources[a].at[:, head_columns(other)],
                    targets[a].at[chip],
                    send_sem.at[a, k],
                    recv_sem.at[a, k],
                    device,
                )
            )
            sent[-1].start()
        kept.append(
            pltpu.make_async_copy(
                sources[a].at[:, head_columns(chip)], targets[a].at[chip], own_sem.at[a]
            )
        )
        kept[-1].start()
        if a < shared:
            passed.append(
                remote(
                    sources[a].at[:, head_columns(chip)],
                    targets[a].at[4 + chip],
                    pass_sem.at[a, 3],
                    passed_sem.at[a, 3],
                    partner,
                )
            )
            passed[-1].start()
    for a in range(count):
        for k, (other, device) in enumerate(peers):
            sent[3 * a + k].wait_recv()
            if a < shared:
                passed.append(
                    remote(
                        targets[a].at[other],
                        targets[a].at[4 + other],
                        pass_sem.at[a, k],
                        passed_sem.at[a, k],
                        partner,
                    )
                )
                passed[-1].start()
    for copy in kept:
        copy.wait()
    for copy in sent:
        copy.wait_send()
    for copy in passed:
        copy.wait()


def spread(arrays, shared, collective_id):
    count = len(arrays)
    rows, columns = arrays[0].shape
    heads = columns // HD
    slots = [2 * heads if a < shared else heads for a in range(count)]
    return pl.pallas_call(
        functools.partial(spread_kernel, shared, count),
        out_shape=tuple(jax.ShapeDtypeStruct((n, rows, HD), jnp.bfloat16) for n in slots),
        in_specs=[ANY_SPEC] * count,
        out_specs=(ANY_SPEC,) * count,
        scratch_shapes=[
            pltpu.SemaphoreType.DMA((count,)),
            pltpu.SemaphoreType.DMA((count, 3)),
            pltpu.SemaphoreType.DMA((count, 3)),
            pltpu.SemaphoreType.DMA((count, 4)),
            pltpu.SemaphoreType.DMA((count, 4)),
        ],
        compiler_params=pltpu.CompilerParams(collective_id=collective_id, has_side_effects=True),
        cost_estimate=cost(8 * count),
        name="spread_heads",
    )(*arrays)


def collect_kernel(source, target, own_sem, send_sem, recv_sem):
    chip, core, peers = chip_peers()
    meet([device for _, device in peers])
    copies = []
    for k, (other, device) in enumerate(peers):
        copies.append(
            remote(
                source.at[other],
                target.at[:, head_columns(chip)],
                send_sem.at[k],
                recv_sem.at[k],
                device,
            )
        )
    copies.append(
        pltpu.make_async_copy(source.at[chip], target.at[:, head_columns(chip)], own_sem)
    )
    for copy in copies:
        copy.start()
    for copy in copies:
        copy.wait()


def collect(array, collective_id):
    heads, rows, _ = array.shape
    return pl.pallas_call(
        collect_kernel,
        out_shape=jax.ShapeDtypeStruct((rows, heads * HD), jnp.bfloat16),
        in_specs=[ANY_SPEC],
        out_specs=ANY_SPEC,
        scratch_shapes=[
            pltpu.SemaphoreType.DMA,
            pltpu.SemaphoreType.DMA((3,)),
            pltpu.SemaphoreType.DMA((3,)),
        ],
        compiler_params=pltpu.CompilerParams(collective_id=collective_id, has_side_effects=True),
        cost_estimate=cost(8),
        name="collect_heads",
    )(array)


def collect_grads_kernel(
    dq_ref,
    dk_ref,
    dv_ref,
    dk_far_ref,
    dv_far_ref,
    query_grad,
    key_grad,
    value_grad,
    near,
    summed,
    pass_sem,
    passed_sem,
    own_sem,
    send_sem,
    recv_sem,
):
    chip, core, peers = chip_peers()
    partner = 2 * chip + 1 - core
    meet([device for _, device in peers] + [partner])
    order = [(k, other, device) for k, (other, device) in enumerate(peers)] + [(3, chip, None)]
    passed, copies = [], []
    for k, other, _ in order:
        for a, far in enumerate((dk_far_ref, dv_far_ref)):
            passed.append(
                remote(
                    far.at[other], near.at[a, other], pass_sem.at[a, k], passed_sem.at[a, k], partner
                )
            )
            passed[-1].start()

    def send(a, source, target, k, other, device):
        place = target.at[:, head_columns(chip)]
        if device is None:
            copies.append(pltpu.make_async_copy(source, place, own_sem.at[a]))
        else:
            copies.append(remote(source, place, send_sem.at[a, k], recv_sem.at[a, k], device))
        copies[-1].start()

    for k, other, device in order:
        send(2, dq_ref.at[other], query_grad, k, other, device)
    for k, other, device in order:
        for a, (share, target) in enumerate(((dk_ref, key_grad), (dv_ref, value_grad))):
            passed[2 * k + a].wait_recv()
            summed[a, other] = (share[other] + near[a, other].astype(jnp.float32)).astype(
                jnp.bfloat16
            )
            send(a, summed.at[a, other], target, k, other, device)
    for copy in passed:
        copy.wait_send()
    for copy in copies:
        copy.wait()


def collect_grads(dq, dk, dv, dk_far, dv_far, collective_id):
    heads, rows, _ = dq.shape
    return pl.pallas_call(
        collect_grads_kernel,
        out_shape=(jax.ShapeDtypeStruct((rows, heads * HD), jnp.bfloat16),) * 3,
        in_specs=[ANY_SPEC, VMEM_SPEC, VMEM_SPEC, ANY_SPEC, ANY_SPEC],
        out_specs=(ANY_SPEC,) * 3,
        scratch_shapes=[
            pltpu.VMEM((2, heads, rows, HD), jnp.bfloat16),
            pltpu.VMEM((2, heads, rows, HD), jnp.bfloat16),
            pltpu.SemaphoreType.DMA((2, 4)),
            pltpu.SemaphoreType.DMA((2, 4)),
            pltpu.SemaphoreType.DMA((3,)),
            pltpu.SemaphoreType.DMA((3, 3)),
            pltpu.SemaphoreType.DMA((3, 3)),
        ],
        compiler_params=pltpu.CompilerParams(
            collective_id=collective_id, has_side_effects=True, vmem_limit_bytes=VMEM_LIMIT
        ),
        cost_estimate=cost(20),
        name="collect_grads",
    )(dq, dk, dv, dk_far, dv_far)


def weight_shares(heads_out, full_grad):
    seq_devices = lax.axis_size("seq")
    share = jnp.einsum("td,tc->dc", full_grad, heads_out, preferred_element_type=jnp.float32)
    width, columns = share.shape
    return share.reshape(seq_devices // 2, 2, width // seq_devices, columns)


def permuted(value, flip):
    pairs = [(source, source ^ flip) for source in range(lax.axis_size("seq"))]
    return lax.ppermute(value, "seq", pairs)


def local_by_heads(
    query_heads,
    key_heads,
    value_heads,
    out_weight,
    cotangent,
    loss_mask,
    block_pattern,
    block_counts,
):
    tok_rows, local_cols = query_heads.shape
    head_count = local_cols // HD
    own_blocks = head_count * tok_rows // BLK
    parity = (lax.axis_index("seq") % 2).astype(jnp.int32).reshape(1)
    masked = jnp.where(loss_mask[:, None] == 1, cotangent, jnp.zeros_like(cotangent))
    full_grad = lax.all_gather(masked, "tp", axis=1, tiled=True)

    keys, values, queries = spread((key_heads, value_heads, query_heads), 2, 0)
    keys = keys.reshape(2 * own_blocks, BLK, HD)
    values = values.reshape(2 * own_blocks, BLK, HD)
    queries = queries.reshape(own_blocks, BLK, HD)

    blocks_bf16 = jax.ShapeDtypeStruct((own_blocks, BLK, HD), jnp.bfloat16)
    blocks_f32 = jax.ShapeDtypeStruct((own_blocks, BLK, HD), jnp.float32)
    heads_blocks, log_total = pl.pallas_call(
        forward_kernel,
        out_shape=(blocks_bf16, jax.ShapeDtypeStruct((own_blocks, 1, BLK), jnp.float32)),
        in_specs=[SMEM_SPEC] * 3 + [VMEM_SPEC] * 3,
        out_specs=(VMEM_SPEC,) * 2,
        scratch_shapes=[pltpu.VMEM((block_pattern.shape[1], BLK, BLK), jnp.float32)],
        compiler_params=pltpu.CompilerParams(vmem_limit_bytes=VMEM_LIMIT),
        cost_estimate=cost(12),
        name="attention_forward",
    )(block_pattern, block_counts, parity, queries, keys, values)
    heads_out = collect(heads_blocks.reshape(head_count, tok_rows, HD), 1)

    partial_out = jnp.dot(heads_out, out_weight, preferred_element_type=jnp.float32)
    partial_out, full_grad = lax.optimization_barrier(
        (partial_out.astype(jnp.bfloat16), full_grad)
    )
    attended = lax.psum_scatter(partial_out, "tp", scatter_dimension=1, tiled=True)
    place = lax.axis_index("seq")
    chip, core = place // 2, place % 2
    d_heads = jnp.einsum(
        "td,cd->tc", full_grad, out_weight, preferred_element_type=jnp.float32
    ).astype(jnp.bfloat16)
    shares = weight_shares(heads_out, full_grad)
    far_share = lax.dynamic_index_in_dim(shares, 1 - core, 1, keepdims=False).astype(jnp.bfloat16)
    near_share = lax.dynamic_index_in_dim(shares, core, 1, keepdims=False)
    d_heads, far_share, near_share = lax.optimization_barrier((d_heads, far_share, near_share))
    both = near_share + permuted(far_share, 1).astype(jnp.float32)
    (grads,) = spread((d_heads,), 0, 2)
    own_piece = lax.dynamic_index_in_dim(both, chip, 0, keepdims=False)
    pieces = [
        lax.dynamic_index_in_dim(both, chip ^ step, 0, keepdims=False).astype(jnp.bfloat16)
        for step in range(1, both.shape[0])
    ]
    grads, own_piece, *pieces = lax.optimization_barrier((grads, own_piece, *pieces))
    arrived = [permuted(piece, 2 * (step + 1)) for step, piece in enumerate(pieces)]
    grads = grads.reshape(own_blocks, BLK, HD)

    dq, dk, dv, dk_far, dv_far = pl.pallas_call(
        backward_kernel,
        out_shape=(blocks_bf16, blocks_f32, blocks_f32, blocks_bf16, blocks_bf16),
        in_specs=[SMEM_SPEC] * 3 + [VMEM_SPEC] * 6,
        out_specs=(VMEM_SPEC,) * 5,
        scratch_shapes=[pltpu.VMEM((2 * own_blocks, BLK, HD), jnp.float32)] * 2,
        compiler_params=pltpu.CompilerParams(vmem_limit_bytes=VMEM_LIMIT),
        cost_estimate=cost(15),
        name="attention_backward",
    )(block_pattern, block_counts, parity, queries, keys, values, heads_blocks, log_total, grads)
    by_source = (head_count, tok_rows, HD)
    query_grad, key_grad, value_grad = collect_grads(
        *(part.reshape(by_source) for part in (dq, dk, dv, dk_far, dv_far)), 3
    )
    weight_grad = own_piece
    for piece in arrived:
        weight_grad = weight_grad + piece.astype(jnp.float32)
    return (attended, query_grad, key_grad, value_grad, weight_grad.T)


def solution(mesh):
    in_specs = (
        P("seq", "tp"),
        P("seq", "tp"),
        P("seq", "tp"),
        P("tp", None),
        P("seq", "tp"),
        P("seq"),
        P(),
        P(),
    )
    out_specs = (P("seq", "tp"), P("seq", "tp"), P("seq", "tp"), P("seq", "tp"), P("tp", "seq"))

    def run(query_heads, *others):
        shard = (
            query_heads.shape[0] // mesh.shape["seq"],
            query_heads.shape[1] // mesh.shape["tp"],
        )
        one_head_a_chip = shard[0] == 2 * BLK and mesh.shape["seq"] == 2 * (shard[1] // HD)
        return jax.shard_map(
            local_by_heads if one_head_a_chip else local,
            mesh=mesh,
            in_specs=in_specs,
            out_specs=out_specs,
            check_vma=False,
        )(query_heads, *others)

    return run
```

```python
import functools
import math

import jax
import jax.numpy as jnp
from jax import lax
from jax.experimental import pallas as pl
from jax.experimental.pallas import tpu as pltpu
from jax.sharding import PartitionSpec as P

HD = 128
BLK = 256
WINDOW = 4


FLOOR_LOGIT = -1e30
SCALE = 1.0 / math.sqrt(HD)
LOG2_SCALE = SCALE * math.log2(math.e)
NT = (((1,), (1,)), ((), ()))
TN = (((0,), (0,)), ((), ()))
VMEM_LIMIT = 48 * 1024 * 1024


def passed_along(value, axis, steps):
    count = lax.axis_size(axis)
    leading, last = (max(0, -steps), min(count, count - steps))
    return lax.ppermute(value, axis, [(source, source + steps) for source in range(leading, last)])


def listed_table(block_pattern, block_counts, query_first, query_count, key_first, key_count):
    query_lists = lax.dynamic_slice_in_dim(block_pattern, query_first, query_count, 0)
    list_sizes = lax.dynamic_slice_in_dim(block_counts, query_first, query_count, 0)
    slot_ids = jnp.arange(block_pattern.shape[1], dtype=jnp.int32)
    in_use = slot_ids[None, :] < list_sizes[:, None]
    key_ids = key_first + jnp.arange(key_count, dtype=jnp.int32)
    matched = (query_lists[:, :, None] == key_ids[None, None, :]) & in_use[:, :, None]
    return jnp.any(matched, axis=1)


def masked_logits(query_part, key_part, listed):
    logits = jnp.einsum(
        "qhd,khd->hqk", query_part, key_part, preferred_element_type=jnp.float32
    ) * (1.0 / math.sqrt(HD))
    head_count, query_len, key_len = logits.shape
    blocked = logits.reshape(
        head_count,
        listed.shape[0],
        query_len // listed.shape[0],
        listed.shape[1],
        key_len // listed.shape[1],
    )
    blocked = jnp.where(listed[None, :, None, :, None], blocked, FLOOR_LOGIT)
    return blocked.reshape(head_count, query_len, key_len)


def piece_logits(query_part, key_part, listed):

    def compute(unused):
        return masked_logits(query_part, key_part, listed)

    def skipped(unused):
        return jnp.full(
            (query_part.shape[1], query_part.shape[0], key_part.shape[0]), FLOOR_LOGIT, jnp.float32
        )

    return lax.cond(jnp.any(listed), compute, skipped, 0)


def piece_output(logits, log_total, value_part, listed):

    def compute(unused):
        weights_b = jnp.exp(logits - log_total[:, :, None]).astype(jnp.bfloat16)
        return jnp.einsum("hqk,khd->hqd", weights_b, value_part, preferred_element_type=jnp.float32)

    def skipped(unused):
        return jnp.zeros((logits.shape[0], logits.shape[1], value_part.shape[2]), jnp.float32)

    return lax.cond(jnp.any(listed), compute, skipped, 0)


def pair_terms(
    logits,
    query_part,
    grad_part,
    log_total,
    row_dots,
    key_part,
    value_part,
    listed,
    want_query,
    want_keys,
):
    query_shape = query_part.shape
    key_shape = key_part.shape

    def compute(unused):
        scores = masked_logits(query_part, key_part, listed) if logits is None else logits
        weights = jnp.exp(scores - log_total[:, :, None])
        d_probs = jnp.einsum(
            "qhd,khd->hqk", grad_part, value_part, preferred_element_type=jnp.float32
        )
        d_logits = (weights * (d_probs - row_dots[:, :, None]) * (1.0 / math.sqrt(HD))).astype(
            jnp.bfloat16
        )
        query_term = jnp.zeros(query_shape, jnp.float32)
        key_term = jnp.zeros(key_shape, jnp.float32)
        value_term = jnp.zeros(key_shape, jnp.float32)
        if want_query:
            query_term = jnp.einsum(
                "hqk,khd->qhd", d_logits, key_part, preferred_element_type=jnp.float32
            )
        if want_keys:
            key_term = jnp.einsum(
                "hqk,qhd->khd", d_logits, query_part, preferred_element_type=jnp.float32
            )
            value_term = jnp.einsum(
                "hqk,qhd->khd",
                weights.astype(jnp.bfloat16),
                grad_part,
                preferred_element_type=jnp.float32,
            )
        return (query_term, key_term, value_term)

    def skipped(unused):
        return (
            jnp.zeros(query_shape, jnp.float32),
            jnp.zeros(key_shape, jnp.float32),
            jnp.zeros(key_shape, jnp.float32),
        )

    return lax.cond(jnp.any(listed), compute, skipped, 0)


def local(
    query_heads,
    key_heads,
    value_heads,
    out_weight,
    cotangent,
    loss_mask,
    block_pattern,
    block_counts,
):
    tok_rows = query_heads.shape[0]
    local_cols = query_heads.shape[1]
    head_count = local_cols // HD
    query_blocks = tok_rows // BLK
    seq_devices = lax.axis_size("seq")
    reach_dev = min((WINDOW * BLK + tok_rows - 1) // tok_rows, seq_devices - 1)
    position = lax.axis_index("seq")
    own_first = position * query_blocks
    query_part = query_heads.reshape(tok_rows, head_count, HD)
    offsets = [distance for distance in range(-reach_dev, reach_dev + 1) if distance != 0]
    neighbours = []
    for distance in offsets:
        arrived = passed_along((key_heads, value_heads), "seq", distance)
        neighbours.append((position - distance, arrived[0], arrived[1]))
    pieces = [(position, key_heads, value_heads)] + neighbours
    prepared = []
    for source, key_piece, value_piece in pieces:
        listed = listed_table(
            block_pattern,
            block_counts,
            own_first,
            query_blocks,
            source * query_blocks,
            query_blocks,
        )
        key_part = key_piece.reshape(tok_rows, head_count, HD)
        value_part = value_piece.reshape(tok_rows, head_count, HD)
        prepared.append((listed, key_part, value_part, piece_logits(query_part, key_part, listed)))
    highest = jnp.full((head_count, tok_rows), FLOOR_LOGIT, jnp.float32)
    for listed, key_part, value_part, logits in prepared:
        highest = jnp.maximum(highest, jnp.max(logits, axis=2))
    denominator = jnp.zeros((head_count, tok_rows), jnp.float32)
    for listed, key_part, value_part, logits in prepared:
        denominator = denominator + jnp.sum(jnp.exp(logits - highest[:, :, None]), axis=2)
    log_total = highest + jnp.log(denominator)
    weighted = jnp.zeros((head_count, tok_rows, HD), jnp.float32)
    for listed, key_part, value_part, logits in prepared:
        weighted = weighted + piece_output(logits, log_total, value_part, listed)
    heads_out = (
        jnp.transpose(weighted, (1, 0, 2)).reshape(tok_rows, local_cols).astype(jnp.bfloat16)
    )
    partial_out = jnp.dot(heads_out, out_weight, preferred_element_type=jnp.float32)
    attended = lax.psum_scatter(partial_out, "tp", scatter_dimension=1, tiled=True).astype(
        jnp.bfloat16
    )
    masked = jnp.where(loss_mask[:, None] == 1, cotangent, jnp.zeros_like(cotangent))
    full_grad = lax.all_gather(masked, "tp", axis=1, tiled=True)
    weight_part = jnp.einsum("tc,td->cd", heads_out, full_grad, preferred_element_type=jnp.float32)
    weight_grad = lax.psum_scatter(weight_part, "seq", scatter_dimension=1, tiled=True)
    d_heads = jnp.einsum(
        "td,cd->tc", full_grad, out_weight, preferred_element_type=jnp.float32
    ).astype(jnp.bfloat16)
    grad_part = d_heads.reshape(tok_rows, head_count, HD)
    row_dots = jnp.sum(
        grad_part.astype(jnp.float32)
        * heads_out.reshape(tok_rows, head_count, HD).astype(jnp.float32),
        axis=2,
    ).T
    own_listed, own_keys, own_values, own_logits = prepared[0]
    term_set = pair_terms(
        own_logits,
        query_part,
        grad_part,
        log_total,
        row_dots,
        own_keys,
        own_values,
        own_listed,
        True,
        True,
    )
    query_acc, key_acc, value_acc = term_set
    for listed, key_part, value_part, logits in prepared[1:]:
        term_set = pair_terms(
            logits,
            query_part,
            grad_part,
            log_total,
            row_dots,
            key_part,
            value_part,
            listed,
            True,
            False,
        )
        query_acc = query_acc + term_set[0]
    for distance in offsets:
        arrived = passed_along((query_heads, d_heads), "seq", distance)
        arrived_stats = passed_along((log_total, row_dots), "seq", distance)
        sender = position - distance
        inside = (sender >= 0) & (sender < seq_devices)
        listed = (
            listed_table(
                block_pattern,
                block_counts,
                sender * query_blocks,
                query_blocks,
                own_first,
                query_blocks,
            )
            & inside
        )
        term_set = pair_terms(
            None,
            arrived[0].reshape(tok_rows, head_count, HD),
            arrived[1].reshape(tok_rows, head_count, HD),
            arrived_stats[0],
            arrived_stats[1],
            own_keys,
            own_values,
            listed,
            False,
            True,
        )
        key_acc = key_acc + term_set[1]
        value_acc = value_acc + term_set[2]
    query_grad = query_acc.reshape(tok_rows, local_cols).astype(jnp.bfloat16)
    key_grad = key_acc.reshape(tok_rows, local_cols).astype(jnp.bfloat16)
    value_grad = value_acc.reshape(tok_rows, local_cols).astype(jnp.bfloat16)
    return (attended, query_grad, key_grad, value_grad, weight_grad)


def block_slot(block, parity):
    return (((block // 2) + parity) % 2) * 8 + (block // 4) * 2 + block % 2


def over_entries(body, entries, state):
    state = lax.fori_loop(
        0, entries // 2, lambda step, state: body(2 * step + 1, body(2 * step, state)), state
    )
    return lax.fori_loop(0, entries % 2, lambda step, state: body(entries - 1, state), state)


def forward_kernel(pattern, counts, parity_ref, q_ref, k_ref, v_ref, out_ref, total_ref, scores):
    parity = parity_ref[0]

    def query_block(index, carry):
        block = 4 * (index // 2) + 2 * parity + index % 2
        entries = counts[block]
        query = q_ref[index]


        def score(entry, highest):
            slot = block_slot(pattern[block, entry], parity)
            logits = (
                lax.dot_general(k_ref[slot], query, NT, preferred_element_type=jnp.float32)
                * LOG2_SCALE
            )
            scores[entry] = logits
            return jnp.maximum(highest, jnp.max(logits, axis=0, keepdims=True))

        highest = over_entries(score, entries, jnp.full((1, BLK), FLOOR_LOGIT, jnp.float32))

        def blend(entry, state):
            total, mixed = state
            slot = block_slot(pattern[block, entry], parity)
            weights = jnp.exp2(scores[entry] - highest)
            total = total + jnp.sum(weights, axis=0, keepdims=True)
            mixed = mixed + lax.dot_general(
                v_ref[slot], weights.astype(jnp.bfloat16), TN, preferred_element_type=jnp.float32
            )
            return total, mixed

        total, mixed = over_entries(
            blend,
            entries,
            (jnp.zeros((1, BLK), jnp.float32), jnp.zeros((HD, BLK), jnp.float32)),
        )
        out_ref[index] = jnp.transpose(mixed / total).astype(jnp.bfloat16)
        total_ref[index] = highest + jnp.log2(total)
        return carry

    lax.fori_loop(0, q_ref.shape[0], query_block, 0)


def backward_kernel(
    pattern,
    counts,
    parity_ref,
    q_ref,
    k_ref,
    v_ref,
    out_ref,
    total_ref,
    grad_ref,
    dq_ref,
    dk_ref,
    dv_ref,
    dk_far_ref,
    dv_far_ref,
    dk_acc,
    dv_acc,
):
    parity = parity_ref[0]
    dk_acc[...] = jnp.zeros_like(dk_acc)
    dv_acc[...] = jnp.zeros_like(dv_acc)

    def query_block(index, carry):
        block = 4 * (index // 2) + 2 * parity + index % 2
        query = q_ref[index]
        grad = grad_ref[index]
        log_total = total_ref[index]
        products = grad.astype(jnp.float32) * out_ref[index].astype(jnp.float32)
        row_dots = jnp.sum(jnp.transpose(products), axis=0, keepdims=True)


        def pair(entry, dq):
            slot = block_slot(pattern[block, entry], parity)
            key = k_ref[slot]
            logits = (
                lax.dot_general(key, query, NT, preferred_element_type=jnp.float32) * LOG2_SCALE
            )
            weights = jnp.exp2(logits - log_total)
            d_probs = lax.dot_general(v_ref[slot], grad, NT, preferred_element_type=jnp.float32)
            d_logits = (weights * (d_probs - row_dots)).astype(jnp.bfloat16)
            dv_acc[slot] += jnp.dot(
                weights.astype(jnp.bfloat16), grad, preferred_element_type=jnp.float32
            )
            dk_acc[slot] += jnp.dot(d_logits, query, preferred_element_type=jnp.float32)
            return dq + lax.dot_general(key, d_logits, TN, preferred_element_type=jnp.float32)

        dq = over_entries(pair, counts[block], jnp.zeros((HD, BLK), jnp.float32))
        dq_ref[index] = jnp.transpose(dq * SCALE).astype(jnp.bfloat16)
        return carry

    lax.fori_loop(0, q_ref.shape[0], query_block, 0)
    half = dk_acc.shape[0] // 2
    dk_ref[...] = dk_acc[:half] * SCALE
    dv_ref[...] = dv_acc[:half]
    dk_far_ref[...] = (dk_acc[half:] * SCALE).astype(jnp.bfloat16)
    dv_far_ref[...] = dv_acc[half:].astype(jnp.bfloat16)


def cost(microseconds):
    return pl.CostEstimate(
        flops=microseconds * 10**9, bytes_accessed=microseconds * 3 * 10**6, transcendentals=0
    )


SMEM_SPEC = pl.BlockSpec(memory_space=pltpu.SMEM)
VMEM_SPEC = pl.BlockSpec(memory_space=pltpu.VMEM)
ANY_SPEC = pl.BlockSpec(memory_space=pl.ANY)


def chip_peers():
    place = lax.axis_index("seq")
    chip, core = place // 2, place % 2
    others = (chip + 1 - 2 * (chip % 2), (chip + 2) % 4, 3 - chip)
    return chip, core, [(other, 2 * other + core) for other in others]


def meet(devices):
    barrier = pltpu.get_barrier_semaphore()
    for device in devices:
        pl.semaphore_signal(
            barrier, inc=1, device_id={"seq": device}, device_id_type=pl.DeviceIdType.MESH
        )
    pl.semaphore_wait(barrier, len(devices))


def remote(source, target, send_sem, recv_sem, device):
    return pltpu.make_async_remote_copy(
        src_ref=source,
        dst_ref=target,
        send_sem=send_sem,
        recv_sem=recv_sem,
        device_id={"seq": device},
        device_id_type=pl.DeviceIdType.MESH,
    )


def head_columns(head):
    return pl.ds(pl.multiple_of(head * HD, HD), HD)


def spread_kernel(shared, count, *refs):
    sources, targets = refs[:count], refs[count : 2 * count]
    own_sem, send_sem, recv_sem, pass_sem, passed_sem = refs[2 * count :]
    chip, core, peers = chip_peers()
    partner = 2 * chip + 1 - core
    meet([device for _, device in peers] + ([partner] if shared else []))
    sent, kept, passed = [], [], []
    for a in range(count):
        for k, (other, device) in enumerate(peers):
            sent.append(
                remote(
                    sources[a].at[:, head_columns(other)],
                    targets[a].at[chip],
                    send_sem.at[a, k],
                    recv_sem.at[a, k],
                    device,
                )
            )
            sent[-1].start()
        kept.append(
            pltpu.make_async_copy(
                sources[a].at[:, head_columns(chip)], targets[a].at[chip], own_sem.at[a]
            )
        )
        kept[-1].start()
        if a < shared:
            passed.append(
                remote(
                    sources[a].at[:, head_columns(chip)],
                    targets[a].at[4 + chip],
                    pass_sem.at[a, 3],
                    passed_sem.at[a, 3],
                    partner,
                )
            )
            passed[-1].start()
    for a in range(count):
        for k, (other, device) in enumerate(peers):
            sent[3 * a + k].wait_recv()
            if a < shared:
                passed.append(
                    remote(
                        targets[a].at[other],
                        targets[a].at[4 + other],
                        pass_sem.at[a, k],
                        passed_sem.at[a, k],
                        partner,
                    )
                )
                passed[-1].start()
    for copy in kept:
        copy.wait()
    for copy in sent:
        copy.wait_send()
    for copy in passed:
        copy.wait()


def spread(arrays, shared, collective_id):
    count = len(arrays)
    rows, columns = arrays[0].shape
    heads = columns // HD
    slots = [2 * heads if a < shared else heads for a in range(count)]
    return pl.pallas_call(
        functools.partial(spread_kernel, shared, count),
        out_shape=tuple(jax.ShapeDtypeStruct((n, rows, HD), jnp.bfloat16) for n in slots),
        in_specs=[ANY_SPEC] * count,
        out_specs=(ANY_SPEC,) * count,
        scratch_shapes=[
            pltpu.SemaphoreType.DMA((count,)),
            pltpu.SemaphoreType.DMA((count, 3)),
            pltpu.SemaphoreType.DMA((count, 3)),
            pltpu.SemaphoreType.DMA((count, 4)),
            pltpu.SemaphoreType.DMA((count, 4)),
        ],
        compiler_params=pltpu.CompilerParams(collective_id=collective_id, has_side_effects=True),
        cost_estimate=cost(8 * count),
        name="spread_heads",
    )(*arrays)


def collect_kernel(source, target, own_sem, send_sem, recv_sem):
    chip, core, peers = chip_peers()
    meet([device for _, device in peers])
    copies = []
    for k, (other, device) in enumerate(peers):
        copies.append(
            remote(
                source.at[other],
                target.at[:, head_columns(chip)],
                send_sem.at[k],
                recv_sem.at[k],
                device,
            )
        )
    copies.append(
        pltpu.make_async_copy(source.at[chip], target.at[:, head_columns(chip)], own_sem)
    )
    for copy in copies:
        copy.start()
    for copy in copies:
        copy.wait()


def collect(array, collective_id):
    heads, rows, _ = array.shape
    return pl.pallas_call(
        collect_kernel,
        out_shape=jax.ShapeDtypeStruct((rows, heads * HD), jnp.bfloat16),
        in_specs=[ANY_SPEC],
        out_specs=ANY_SPEC,
        scratch_shapes=[
            pltpu.SemaphoreType.DMA,
            pltpu.SemaphoreType.DMA((3,)),
            pltpu.SemaphoreType.DMA((3,)),
        ],
        compiler_params=pltpu.CompilerParams(collective_id=collective_id, has_side_effects=True),
        cost_estimate=cost(8),
        name="collect_heads",
    )(array)


def collect_grads_kernel(
    dq_ref,
    dk_ref,
    dv_ref,
    dk_far_ref,
    dv_far_ref,
    query_grad,
    key_grad,
    value_grad,
    near,
    summed,
    pass_sem,
    passed_sem,
    own_sem,
    send_sem,
    recv_sem,
):
    chip, core, peers = chip_peers()
    partner = 2 * chip + 1 - core
    meet([device for _, device in peers] + [partner])
    order = [(k, other, device) for k, (other, device) in enumerate(peers)] + [(3, chip, None)]
    passed, copies = [], []
    for k, other, _ in order:
        for a, far in enumerate((dk_far_ref, dv_far_ref)):
            passed.append(
                remote(
                    far.at[other], near.at[a, other], pass_sem.at[a, k], passed_sem.at[a, k], partner
                )
            )
            passed[-1].start()

    def send(a, source, target, k, other, device):
        place = target.at[:, head_columns(chip)]
        if device is None:
            copies.append(pltpu.make_async_copy(source, place, own_sem.at[a]))
        else:
            copies.append(remote(source, place, send_sem.at[a, k], recv_sem.at[a, k], device))
        copies[-1].start()

    for k, other, device in order:
        send(2, dq_ref.at[other], query_grad, k, other, device)
    for k, other, device in order:
        for a, (share, target) in enumerate(((dk_ref, key_grad), (dv_ref, value_grad))):
            passed[2 * k + a].wait_recv()
            summed[a, other] = (share[other] + near[a, other].astype(jnp.float32)).astype(
                jnp.bfloat16
            )
            send(a, summed.at[a, other], target, k, other, device)
    for copy in passed:
        copy.wait_send()
    for copy in copies:
        copy.wait()


def collect_grads(dq, dk, dv, dk_far, dv_far, collective_id):
    heads, rows, _ = dq.shape
    return pl.pallas_call(
        collect_grads_kernel,
        out_shape=(jax.ShapeDtypeStruct((rows, heads * HD), jnp.bfloat16),) * 3,
        in_specs=[ANY_SPEC, VMEM_SPEC, VMEM_SPEC, ANY_SPEC, ANY_SPEC],
        out_specs=(ANY_SPEC,) * 3,
        scratch_shapes=[
            pltpu.VMEM((2, heads, rows, HD), jnp.bfloat16),
            pltpu.VMEM((2, heads, rows, HD), jnp.bfloat16),
            pltpu.SemaphoreType.DMA((2, 4)),
            pltpu.SemaphoreType.DMA((2, 4)),
            pltpu.SemaphoreType.DMA((3,)),
            pltpu.SemaphoreType.DMA((3, 3)),
            pltpu.SemaphoreType.DMA((3, 3)),
        ],
        compiler_params=pltpu.CompilerParams(
            collective_id=collective_id, has_side_effects=True, vmem_limit_bytes=VMEM_LIMIT
        ),
        cost_estimate=cost(20),
        name="collect_grads",
    )(dq, dk, dv, dk_far, dv_far)


def weight_shares(heads_out, full_grad):
    seq_devices = lax.axis_size("seq")
    share = jnp.einsum("td,tc->dc", full_grad, heads_out, preferred_element_type=jnp.float32)
    width, columns = share.shape
    return share.reshape(seq_devices // 2, 2, width // seq_devices, columns)


def permuted(value, flip):
    pairs = [(source, source ^ flip) for source in range(lax.axis_size("seq"))]
    return lax.ppermute(value, "seq", pairs)


def local_by_heads(
    query_heads,
    key_heads,
    value_heads,
    out_weight,
    cotangent,
    loss_mask,
    block_pattern,
    block_counts,
):
    tok_rows, local_cols = query_heads.shape
    head_count = local_cols // HD
    own_blocks = head_count * tok_rows // BLK
    parity = (lax.axis_index("seq") % 2).astype(jnp.int32).reshape(1)
    masked = jnp.where(loss_mask[:, None] == 1, cotangent, jnp.zeros_like(cotangent))
    full_grad = lax.all_gather(masked, "tp", axis=1, tiled=True)

    keys, values, queries = spread((key_heads, value_heads, query_heads), 2, 0)
    keys = keys.reshape(2 * own_blocks, BLK, HD)
    values = values.reshape(2 * own_blocks, BLK, HD)
    queries = queries.reshape(own_blocks, BLK, HD)

    blocks_bf16 = jax.ShapeDtypeStruct((own_blocks, BLK, HD), jnp.bfloat16)
    blocks_f32 = jax.ShapeDtypeStruct((own_blocks, BLK, HD), jnp.float32)
    heads_blocks, log_total = pl.pallas_call(
        forward_kernel,
        out_shape=(blocks_bf16, jax.ShapeDtypeStruct((own_blocks, 1, BLK), jnp.float32)),
        in_specs=[SMEM_SPEC] * 3 + [VMEM_SPEC] * 3,
        out_specs=(VMEM_SPEC,) * 2,
        scratch_shapes=[pltpu.VMEM((block_pattern.shape[1], BLK, BLK), jnp.float32)],
        compiler_params=pltpu.CompilerParams(vmem_limit_bytes=VMEM_LIMIT),
        cost_estimate=cost(12),
        name="attention_forward",
    )(block_pattern, block_counts, parity, queries, keys, values)
    heads_out = collect(heads_blocks.reshape(head_count, tok_rows, HD), 1)

    partial_out = jnp.dot(heads_out, out_weight, preferred_element_type=jnp.float32)
    partial_out, full_grad = lax.optimization_barrier(
        (partial_out.astype(jnp.bfloat16), full_grad)
    )
    attended = lax.psum_scatter(partial_out, "tp", scatter_dimension=1, tiled=True)
    place = lax.axis_index("seq")
    chip, core = place // 2, place % 2
    d_heads = jnp.einsum(
        "td,cd->tc", full_grad, out_weight, preferred_element_type=jnp.float32
    ).astype(jnp.bfloat16)
    shares = weight_shares(heads_out, full_grad)
    far_share = lax.dynamic_index_in_dim(shares, 1 - core, 1, keepdims=False).astype(jnp.bfloat16)
    d_heads, far_share, shares = lax.optimization_barrier((d_heads, far_share, shares))
    near_share = lax.dynamic_index_in_dim(shares, core, 1, keepdims=False)
    both = near_share + permuted(far_share, 1).astype(jnp.float32)
    (grads,) = spread((d_heads,), 0, 2)
    own_piece = lax.dynamic_index_in_dim(both, chip, 0, keepdims=False)
    pieces = [
        lax.dynamic_index_in_dim(both, chip ^ step, 0, keepdims=False).astype(jnp.bfloat16)
        for step in range(1, both.shape[0])
    ]
    grads, own_piece, *pieces = lax.optimization_barrier((grads, own_piece, *pieces))
    arrived = [permuted(piece, 2 * (step + 1)) for step, piece in enumerate(pieces)]
    grads = grads.reshape(own_blocks, BLK, HD)

    dq, dk, dv, dk_far, dv_far = pl.pallas_call(
        backward_kernel,
        out_shape=(blocks_bf16, blocks_f32, blocks_f32, blocks_bf16, blocks_bf16),
        in_specs=[SMEM_SPEC] * 3 + [VMEM_SPEC] * 6,
        out_specs=(VMEM_SPEC,) * 5,
        scratch_shapes=[pltpu.VMEM((2 * own_blocks, BLK, HD), jnp.float32)] * 2,
        compiler_params=pltpu.CompilerParams(vmem_limit_bytes=VMEM_LIMIT),
        cost_estimate=cost(15),
        name="attention_backward",
    )(block_pattern, block_counts, parity, queries, keys, values, heads_blocks, log_total, grads)
    by_source = (head_count, tok_rows, HD)
    query_grad, key_grad, value_grad = collect_grads(
        *(part.reshape(by_source) for part in (dq, dk, dv, dk_far, dv_far)), 3
    )
    weight_grad = own_piece
    for piece in arrived:
        weight_grad = weight_grad + piece.astype(jnp.float32)
    return (attended, query_grad, key_grad, value_grad, weight_grad.T)


def solution(mesh):
    in_specs = (
        P("seq", "tp"),
        P("seq", "tp"),
        P("seq", "tp"),
        P("tp", None),
        P("seq", "tp"),
        P("seq"),
        P(),
        P(),
    )
    out_specs = (P("seq", "tp"), P("seq", "tp"), P("seq", "tp"), P("seq", "tp"), P("tp", "seq"))

    def run(query_heads, *others):
        shard = (
            query_heads.shape[0] // mesh.shape["seq"],
            query_heads.shape[1] // mesh.shape["tp"],
        )
        one_head_a_chip = shard[0] == 2 * BLK and mesh.shape["seq"] == 2 * (shard[1] // HD)
        return jax.shard_map(
            local_by_heads if one_head_a_chip else local,
            mesh=mesh,
            in_specs=in_specs,
            out_specs=out_specs,
            check_vma=False,
        )(query_heads, *others)

    return run
```
